32 devices in a mesh: dp: 8 (over y, x, core), mp: 4 (over z).
Axes of the slice: x: 2, y: 2, z: 4, core: 2. Of those that a mesh axis runs over, the one named last changes fastest.
Arguments:
- qkv_weight: float32 [2, 3, 768, 768], P(None, None, 'dp', 'mp'), may hold values from -0.21875 to 0.21875
- qkv_first: float32 [2, 3, 768, 768], P(None, None, 'dp', 'mp'), may hold values from -2.861023e-06 to 2.861023e-06
- qkv_second: float32 [2, 3, 768, 768], P(None, None, 'dp', 'mp'), may hold values from 2.001037e-13 to 3.1723758e-12
- out_weight: float32 [2, 768, 768], P(None, 'mp', 'dp'), may hold values from -0.875 to 0.875
- out_first: float32 [2, 768, 768], P(None, 'mp', 'dp'), may hold values from -2.861023e-06 to 2.861023e-06
- out_second: float32 [2, 768, 768], P(None, 'mp', 'dp'), may hold values from 2.001037e-13 to 3.1723758e-12
- up_weight: float32 [2, 768, 3072], P(None, 'dp', 'mp'), may hold values from -0.21875 to 0.21875
- up_first: float32 [2, 768, 3072], P(None, 'dp', 'mp'), may hold values from -2.861023e-06 to 2.861023e-06
- up_second: float32 [2, 768, 3072], P(None, 'dp', 'mp'), may hold values from 2.001037e-13 to 3.1723758e-12
- down_weight: float32 [2, 3072, 768], P(None, 'mp', 'dp'), may hold values from -0.109375 to 0.109375
- down_first: float32 [2, 3072, 768], P(None, 'mp', 'dp'), may hold values from -2.861023e-06 to 2.861023e-06
- down_second: float32 [2, 3072, 768], P(None, 'mp', 'dp'), may hold values from 2.001037e-13 to 3.1723758e-12
- code_table: float32 [8192, 768], P('mp', 'dp')
- table_first: float32 [8192, 768], P('mp', 'dp'), may hold values from -2.861023e-06 to 2.861023e-06
- table_second: float32 [8192, 768], P('mp', 'dp'), may hold values from 2.001037e-13 to 3.1723758e-12
- small_params: float32 [42144], replicated
- small_first: float32 [42144], replicated, may hold values from -2.861023e-06 to 2.861023e-06
- small_second: float32 [42144], replicated, may hold values from 2.001037e-13 to 3.1723758e-12
- patch_codes: int32 [64, 196], P('dp'), may hold values from 0 to 8191
- masked_pos: int32 [64, 75], P('dp'), may hold values from 0 to 195, as said below
- masked_count: int32 [64], P('dp'), may hold values from 1 to 75, as said below
Outputs:
- qkv_weight_new: float32 [2, 3, 768, 768], P(None, None, 'dp', 'mp')
- qkv_first_new: float32 [2, 3, 768, 768], P(None, None, 'dp', 'mp')
- qkv_second_new: float32 [2, 3, 768, 768], P(None, None, 'dp', 'mp')
- out_weight_new: float32 [2, 768, 768], P(None, 'mp', 'dp')
- out_first_new: float32 [2, 768, 768], P(None, 'mp', 'dp')
- out_second_new: float32 [2, 768, 768], P(None, 'mp', 'dp')
- up_weight_new: float32 [2, 768, 3072], P(None, 'dp', 'mp')
- up_first_new: float32 [2, 768, 3072], P(None, 'dp', 'mp')
- up_second_new: float32 [2, 768, 3072], P(None, 'dp', 'mp')
- down_weight_new: float32 [2, 3072, 768], P(None, 'mp', 'dp')
- down_first_new: float32 [2, 3072, 768], P(None, 'mp', 'dp')
- down_second_new: float32 [2, 3072, 768], P(None, 'mp', 'dp')
- code_table_new: float32 [8192, 768], P('mp', 'dp')
- table_first_new: float32 [8192, 768], P('mp', 'dp')
- table_second_new: float32 [8192, 768], P('mp', 'dp')
- small_params_new: float32 [42144], replicated
- small_first_new: float32 [42144], replicated
- small_second_new: float32 [42144], replicated
- loss_sum: float32 [], replicated
- masked_total: float32 [], replicated
- grad_norm: float32 [], replicated
The draws below stay inside these ranges and needn't reach their ends.
Inputs may be any that keep to these rules, and one draw needn't show every extreme that they name: `masked_pos`: each row lists 75 different patch numbers of its image. An image's masked patches are the first masked_count entries of its row of masked_pos.
All inputs are finite; a program needn't handle non-finite values.
Results may differ from the reference program's by a relative error of at most 0.0025.
The reference program's roundings to bfloat16 on the way count: a program that leaves them out, or rounds other values in their place, can miss the bound.
Values may be sent and summed in bfloat16 or wider, within the bound.
A program may use at most 256 MiB of HBM per device.

```python
import math
import jax
import jax.numpy as jnp
import numpy as np
from jax import lax

D = 768
H = 12
DH = 64
FF = 3072
V = 8192
GRID = 14
LAYERS = 2
MAXM = 75
STEP = 10
SEQ = 197
PATCH = 196
NREL = 732
IMAGES = 64
NSMALL = 42144
PARAMS = 20489376


def draw_code_table(key, part):
    row_index = jnp.arange(V, dtype=jnp.float32)[:, None] / (V - 1)
    entries = jax.random.normal(key, (V, D), jnp.float32)
    rising = 1.0 + 2.0 * row_index
    return entries * rising * D ** (-0.5)


def draw_small_params(key, part):
    subkeys = jax.random.split(key, 8)

    def draw_noise(subkey, array_shape):
        return jax.random.normal(subkey, array_shape, jnp.float32)
    rising = 0.5 + jnp.arange(D, dtype=jnp.float32) / D
    gain_rows = rising * (1.0 + 0.1 * draw_noise(subkeys[0], (LAYERS, 2, D)))
    biases = 0.1 * draw_noise(subkeys[1], (LAYERS, 6, D))
    scales = jnp.exp(jax.random.uniform(subkeys[2], (LAYERS, 2, D), jnp.float32, -0.7, 0.4))
    vectors = jnp.stack([gain_rows[:, 0], biases[:, 0], biases[:, 1], biases[:, 2], biases[:, 3], scales[:, 0], gain_rows[:, 1], biases[:, 4], biases[:, 5], scales[:, 1]], 1)
    fc_bias = 0.1 * draw_noise(subkeys[3], (LAYERS, FF))
    rel_tables = 0.5 * draw_noise(subkeys[4], (LAYERS, H, NREL))
    special_tokens = draw_noise(subkeys[5], (2, D))
    final_gain = rising * (1.0 + 0.1 * draw_noise(subkeys[6], (D,)))
    final_shift = 0.1 * draw_noise(subkeys[7], (D,))
    return jnp.concatenate([vectors.reshape(-1), fc_bias.reshape(-1), rel_tables.reshape(-1), special_tokens.reshape(-1), final_gain, final_shift])


def draw_masked_pos(key, part):
    subkeys = jax.random.split(key, IMAGES)
    return jax.vmap(lambda k: jax.random.permutation(k, PATCH)[:MAXM])(subkeys).astype(jnp.int32)


def draw_masked_count(key, part):
    image_index = jnp.arange(IMAGES)
    floor_count = MAXM // 3
    base_count = floor_count + (MAXM - floor_count) * (image_index + 1) // IMAGES
    jitter = jax.random.randint(key, (IMAGES,), 0, MAXM // 8 + 2)
    jitter = jnp.where(image_index == IMAGES - 1, 0, jitter)
    return jnp.clip(base_count - jitter, 1, MAXM).astype(jnp.int32)


def place_ends(result, own_key, low, top_value):
    spot = [jax.random.randint(jax.random.fold_in(own_key, axis), (), 0, length) for axis, length in enumerate(result.shape)]
    widest = result.shape.index(max(result.shape))
    next_to = spot[:widest] + [(spot[widest] + 1) % result.shape[widest]] + spot[widest + 1:]
    return result.at[tuple(spot)].set(low).at[tuple(next_to)].set(top_value)


def block_scale(own_key, dims, shards, smallest, high):
    level = 1.0
    for axis_at, parts in shards:
        draws = jax.random.uniform(jax.random.fold_in(jax.random.fold_in(own_key, 6), axis_at), (parts,), jnp.float32, smallest / len(shards), high / len(shards))
        level = level * jnp.repeat(jnp.exp(draws), dims[axis_at] // parts).reshape((-1,) + (1,) * (len(dims) - 1 - axis_at))
    return level


def cumulative_ranks(number_of, skew):
    portions = [(1 << 20) // math.isqrt(standing ** skew) + 1 for standing in range(1, number_of + 1)]
    scale = 1 + sum(portions) // (1 << 30)
    return np.cumsum(np.array([max(1, weight // scale) for weight in portions]))


def ranked_ids(own_key, shape, number_of, slope):
    grid = cumulative_ranks(number_of, slope)
    lot = jax.random.randint(jax.random.fold_in(own_key, 1), shape, 0, int(grid[number_of - 1]))
    grade = jnp.searchsorted(jnp.asarray(grid, jnp.int32), lot, side="right")
    return jax.random.permutation(jax.random.fold_in(own_key, 2), number_of)[grade].astype(jnp.int32)


def normal_values(rng, dims, scale, reach, cuts=(), kind=jnp.bfloat16):
    values = scale * jax.random.normal(rng, dims, jnp.float32)
    if cuts:
        values = values * block_scale(rng, dims, cuts, -0.22, 0.18)
    return jnp.clip(values, -reach, reach).astype(kind)


def setup_inputs(seed: int = 0) -> dict:
    key_list = jax.random.split(jax.random.key(seed), 22)
    qkv_weight = normal_values(key_list[0], (LAYERS, 3, D, D), D ** -0.5, 0.21875, ((2, 8), (3, 4)), jnp.float32)
    qkv_first = normal_values(key_list[1], (LAYERS, 3, D, D), (0.0022 / PARAMS ** 0.5), 2.86102294921875e-06, ((2, 8), (3, 4)), jnp.float32)
    qkv_second = jnp.clip(jnp.exp(math.log(3.1723757735330205e-12) - 2.7634003 * jax.random.uniform(key_list[2], (LAYERS, 3, D, D), jnp.float32) ** block_scale(key_list[2], (LAYERS, 3, D, D), ((2, 8), (3, 4)), -0.2, 0.2)), 2.0010370042813225e-13, 3.1723757735330205e-12)
    out_weight = normal_values(key_list[3], (LAYERS, D, D), (D // 16) ** -0.5, 0.875, ((1, 4), (2, 8)), jnp.float32)
    out_first = normal_values(key_list[4], (LAYERS, D, D), (0.0022 / PARAMS ** 0.5), 2.86102294921875e-06, ((1, 4), (2, 8)), jnp.float32)
    out_second = jnp.clip(jnp.exp(math.log(3.1723757735330205e-12) - 2.7634003 * jax.random.uniform(key_list[5], (LAYERS, D, D), jnp.float32) ** block_scale(key_list[5], (LAYERS, D, D), ((1, 4), (2, 8)), -0.2, 0.2)), 2.0010370042813225e-13, 3.1723757735330205e-12)
    up_weight = normal_values(key_list[6], (LAYERS, D, FF), D ** -0.5, 0.21875, ((1, 8), (2, 4)), jnp.float32)
    up_first = normal_values(key_list[7], (LAYERS, D, FF), (0.0022 / PARAMS ** 0.5), 2.86102294921875e-06, ((1, 8), (2, 4)), jnp.float32)
    up_second = jnp.clip(jnp.exp(math.log(3.1723757735330205e-12) - 2.7634003 * jax.random.uniform(key_list[8], (LAYERS, D, FF), jnp.float32) ** block_scale(key_list[8], (LAYERS, D, FF), ((1, 8), (2, 4)), -0.2, 0.2)), 2.0010370042813225e-13, 3.1723757735330205e-12)
    down_weight = normal_values(key_list[9], (LAYERS, FF, D), FF ** -0.5, 0.109375, ((1, 4), (2, 8)), jnp.float32)
    down_first = normal_values(key_list[10], (LAYERS, FF, D), (0.0022 / PARAMS ** 0.5), 2.86102294921875e-06, ((1, 4), (2, 8)), jnp.float32)
    down_second = jnp.clip(jnp.exp(math.log(3.1723757735330205e-12) - 2.7634003 * jax.random.uniform(key_list[11], (LAYERS, FF, D), jnp.float32) ** block_scale(key_list[11], (LAYERS, FF, D), ((1, 4), (2, 8)), -0.2, 0.2)), 2.0010370042813225e-13, 3.1723757735330205e-12)
    code_table = draw_code_table(jax.random.fold_in(key_list[21], 71), 0)
    table_first = normal_values(key_list[13], (V, D), (0.0022 / PARAMS ** 0.5), 2.86102294921875e-06, ((0, 4), (1, 8)), jnp.float32)
    table_second = jnp.clip(jnp.exp(math.log(3.1723757735330205e-12) - 2.7634003 * jax.random.uniform(key_list[14], (V, D), jnp.float32) ** block_scale(key_list[14], (V, D), ((0, 4), (1, 8)), -0.2, 0.2)), 2.0010370042813225e-13, 3.1723757735330205e-12)
    small_params = draw_small_params(jax.random.fold_in(key_list[21], 71), 0)
    small_first = normal_values(key_list[16], (NSMALL,), (0.0022 / PARAMS ** 0.5), 2.86102294921875e-06, (), jnp.float32)
    small_second = jnp.clip(jnp.exp(jax.random.uniform(key_list[17], (NSMALL,), jnp.float32, math.log(2.0010370042813225e-13), math.log(3.1723757735330205e-12))), 2.0010370042813225e-13, 3.1723757735330205e-12)
    patch_codes = place_ends(ranked_ids(key_list[18], (IMAGES, PATCH), V, 2), jax.random.fold_in(key_list[18], 3), 0, V - 1).astype(jnp.int32)
    masked_pos = draw_masked_pos(jax.random.fold_in(key_list[21], 71), 0)
    masked_count = draw_masked_count(jax.random.fold_in(key_list[21], 71), 0)
    return dict(qkv_weight=qkv_weight, qkv_first=qkv_first, qkv_second=qkv_second, out_weight=out_weight, out_first=out_first, out_second=out_second, up_weight=up_weight, up_first=up_first, up_second=up_second, down_weight=down_weight, down_first=down_first, down_second=down_second, code_table=code_table, table_first=table_first, table_second=table_second, small_params=small_params, small_first=small_first, small_second=small_second, patch_codes=patch_codes, masked_pos=masked_pos, masked_count=masked_count)


HIGHEST = lax.Precision.HIGHEST
NORM_EPS = 1e-06
CLIP_NORM = 0.02
LEARN_RATE = 0.03
BETA_ONE = 0.9
BETA_TWO = 0.98
ADAM_EPS = 1e-08
WEIGHT_DECAY = 0.05

@jax.custom_vjp
def low(v):
    return lax.optimization_barrier(v.astype(jnp.bfloat16)).astype(jnp.float32)

@jax.custom_vjp
def low_back(v):
    return v

def low_keep(v):
    return (low(v), None)

def low_pass(kept, grad):
    return (grad,)

def back_keep(v):
    return (v, None)

def back_low(kept, grad):
    return (low(grad),)
low.defvjp(low_keep, low_pass)
low_back.defvjp(back_keep, back_low)

def rounded_both(values):
    return low_back(low(values))

def rel_index(grid_side):
    extent = 2 * grid_side - 1
    coords = np.stack(np.meshgrid(np.arange(grid_side), np.arange(grid_side), indexing='ij')).reshape(2, -1)
    offsets = coords[:, :, None] - coords[:, None, :] + grid_side - 1
    inner_index = offsets[0] * extent + offsets[1]
    seq_len = grid_side * grid_side + 1
    top_row = np.concatenate([np.full((1, 1), extent * extent + 2), np.full((1, seq_len - 1), extent * extent)], 1)
    lower_rows = np.concatenate([np.full((seq_len - 1, 1), extent * extent + 1), inner_index], 1)
    return np.concatenate([top_row, lower_rows], 0).astype(np.int32)

def unpack_small(packed):
    first_end = LAYERS * 10 * D
    second_end = first_end + LAYERS * FF
    third_end = second_end + LAYERS * H * NREL
    vectors = packed[:first_end].reshape(LAYERS, 10, D)
    fc_bias = packed[first_end:second_end].reshape(LAYERS, FF)
    rel_tables = packed[second_end:third_end].reshape(LAYERS, H, NREL)
    special = packed[third_end:].reshape(4, D)
    return (vectors, fc_bias, rel_tables, special)

def layer_norm(values, gain_vec, shift_vec):
    average = lax.optimization_barrier(jnp.mean(values, -1, keepdims=True))
    centred = values - average
    variance = lax.optimization_barrier(jnp.mean(centred * centred, -1, keepdims=True))
    return centred * lax.rsqrt(variance + NORM_EPS) * gain_vec + shift_vec

def softmax_rows(scores):
    highest = lax.optimization_barrier(jnp.max(scores, -1, keepdims=True))
    exponent = jnp.exp(scores - highest)
    return exponent / lax.optimization_barrier(jnp.sum(exponent, -1, keepdims=True))

def adam_update(weight, moment_one, moment_two, gradient, factor, decay_rate):
    clipped = gradient * factor
    new_first = BETA_ONE * moment_one + (1.0 - BETA_ONE) * clipped
    new_second = BETA_TWO * moment_two + (1.0 - BETA_TWO) * clipped * clipped
    direction = new_first / (1.0 - BETA_ONE ** STEP) / (jnp.sqrt(new_second / (1.0 - BETA_TWO ** STEP)) + ADAM_EPS)
    return (weight - LEARN_RATE * (direction + decay_rate * weight), new_first, new_second)

def model_loss(qkv_weight, out_weight, up_weight, down_weight, code_table, small_params, patch_codes, masked_pos, masked_count):
    vectors, fc_bias, rel_tables, special = unpack_small(small_params)
    table_low = low(code_table)
    qkv_low = low(qkv_weight)
    out_low = low(out_weight)
    up_low = low(up_weight)
    down_low = low(down_weight)
    rel_map = rel_index(GRID)
    per_group = math.gcd(IMAGES, 16)
    groups = IMAGES // per_group
    score_scale = DH ** (-0.5)
    head_shape = (per_group, SEQ, H, DH)

    def one_layer(x, l):
        layer_vec = vectors[l]
        normed = low(layer_norm(x, layer_vec[0], layer_vec[1]))
        query_rows = rounded_both(jnp.dot(normed, qkv_low[l, 0], precision=HIGHEST) + layer_vec[2])
        key_rows = rounded_both(jnp.dot(normed, qkv_low[l, 1], precision=HIGHEST))
        value_rows = rounded_both(jnp.dot(normed, qkv_low[l, 2], precision=HIGHEST) + layer_vec[3])
        raw_scores = jnp.einsum('bqhd,bkhd->bhqk', query_rows.reshape(head_shape), key_rows.reshape(head_shape), precision=HIGHEST)
        attn_probs = softmax_rows(low_back(raw_scores * score_scale + rel_tables[l][:, rel_map][None]))
        mixed_heads = rounded_both(jnp.einsum('bhqk,bkhd->bqhd', low(attn_probs), value_rows.reshape(head_shape), precision=HIGHEST).reshape(-1, D))
        attn_out = low_back(jnp.dot(mixed_heads, out_low[l], precision=HIGHEST) + layer_vec[4])
        x_mid = x + layer_vec[5] * attn_out
        normed_mlp = low(layer_norm(x_mid, layer_vec[6], layer_vec[7]))
        pre_act = low_back(jnp.dot(normed_mlp, up_low[l], precision=HIGHEST) + fc_bias[l])
        activated = low(jax.nn.gelu(pre_act, approximate=False))
        mlp_out = low_back(jnp.dot(activated, down_low[l], precision=HIGHEST) + layer_vec[8])
        return x_mid + layer_vec[9] * mlp_out

    def group_loss(running, block_data):
        image_codes, masked_spots, counts = block_data
        valid_slots = jnp.arange(MAXM)[None, :] < counts[:, None]
        hidden_patch = jnp.any((masked_spots[:, :, None] == jnp.arange(PATCH)[None, None, :]) & valid_slots[:, :, None], 1)
        embedded = low_back(jnp.take(table_low, image_codes, axis=0))
        patches = jnp.where(hidden_patch[:, :, None], special[1], embedded)
        x = jnp.concatenate([jnp.broadcast_to(special[0], (per_group, 1, D)), patches], 1).reshape(-1, D)
        for l in range(LAYERS):
            x = one_layer(x, l)
        normed = low(layer_norm(x, special[2], special[3])).reshape(per_group, SEQ, D)
        picked = jnp.take_along_axis(normed[:, 1:], masked_spots[:, :, None], 1).reshape(-1, D)
        logits = low_back(jnp.dot(picked, table_low.T, precision=HIGHEST))
        highest = lax.optimization_barrier(jnp.max(logits, -1))
        log_total = highest + jnp.log(lax.optimization_barrier(jnp.sum(jnp.exp(logits - highest[:, None]), -1)))
        targets = jnp.take_along_axis(image_codes, masked_spots, 1).reshape(-1)
        target_logit = jnp.take_along_axis(logits, targets[:, None], 1)[:, 0]
        terms = (log_total - target_logit) * valid_slots.reshape(-1).astype(jnp.float32)
        return (running + jnp.sum(terms), None)
    blocks = (patch_codes.reshape(groups, per_group, PATCH), masked_pos.reshape(groups, per_group, MAXM), masked_count.reshape(groups, per_group))
    loss_sum, unused = lax.scan(jax.checkpoint(group_loss), jnp.zeros((), jnp.float32), blocks)
    return loss_sum

def reference(qkv_weight, qkv_first, qkv_second, out_weight, out_first, out_second, up_weight, up_first, up_second, down_weight, down_first, down_second, code_table, table_first, table_second, small_params, small_first, small_second, patch_codes, masked_pos, masked_count):
    count_total = jnp.sum(masked_count).astype(jnp.float32)

    def objective(qkv_arg, out_arg, up_arg, down_arg, table_arg, small_arg):
        return model_loss(qkv_arg, out_arg, up_arg, down_arg, table_arg, small_arg, patch_codes, masked_pos, masked_count)
    loss_sum, pullback = jax.vjp(objective, qkv_weight, out_weight, up_weight, down_weight, code_table, small_params)
    gradients = pullback(jnp.ones((), jnp.float32) / count_total)
    grad_norm = jnp.sqrt(sum((jnp.sum(g * g) for g in gradients)))
    factor = jnp.minimum(1.0, CLIP_NORM / (grad_norm + 1e-06))
    qkv_new, qkv_one, qkv_two = adam_update(qkv_weight, qkv_first, qkv_second, gradients[0], factor, WEIGHT_DECAY)
    out_new, out_one, out_two = adam_update(out_weight, out_first, out_second, gradients[1], factor, WEIGHT_DECAY)
    up_new, up_one, up_two = adam_update(up_weight, up_first, up_second, gradients[2], factor, WEIGHT_DECAY)
    down_new, down_one, down_two = adam_update(down_weight, down_first, down_second, gradients[3], factor, WEIGHT_DECAY)
    table_new, table_one, table_two = adam_update(code_table, table_first, table_second, gradients[4], factor, WEIGHT_DECAY)
    small_new, small_one, small_two = adam_update(small_params, small_first, small_second, gradients[5], factor, 0.0)
    return (qkv_new, qkv_one, qkv_two, out_new, out_one, out_two, up_new, up_one, up_two, down_new, down_one, down_two, table_new, table_one, table_two, small_new, small_one, small_two, loss_sum, count_total, grad_norm)
```

```python
import functools

import jax
import jax.numpy as jnp
from jax import lax
from jax.experimental import pallas as pl
from jax.experimental.pallas import tpu as pltpu
from jax.sharding import PartitionSpec as P

D = 768
H = 12
DH = 64
FF = 3072
V = 8192
GRID = 14
LAYERS = 2
MAXM = 75
STEP = 10
SEQ = 197
PATCH = 196
NREL = 732


MESH = pl.DeviceIdType.MESH
HIGHEST = lax.Precision.HIGHEST
NORM_EPS = 1e-06
CLIP_NORM = 0.02
LEARN_RATE = 0.03
BETA_ONE = 0.9
BETA_TWO = 0.98
ADAM_EPS = 1e-08
WEIGHT_DECAY = 0.05


def unpack_small(packed):
    first_end = LAYERS * 10 * D
    second_end = first_end + LAYERS * FF
    third_end = second_end + LAYERS * H * NREL
    vectors = packed[:first_end].reshape(LAYERS, 10, D)
    fc_bias = packed[first_end:second_end].reshape(LAYERS, FF)
    rel_tables = packed[second_end:third_end].reshape(LAYERS, H, NREL)
    special = packed[third_end:].reshape(4, D)
    return (vectors, fc_bias, rel_tables, special)


def pack_small(vectors, fc_bias, rel_tables, special):
    return jnp.concatenate(
        [vectors.reshape(-1), fc_bias.reshape(-1), rel_tables.reshape(-1), special.reshape(-1)]
    )


def layer_norm(values, gain_vec, shift_vec):
    average = jnp.mean(values, -1, keepdims=True)
    centred = values - average
    variance = jnp.mean(centred * centred, -1, keepdims=True)
    return centred * lax.rsqrt(variance + NORM_EPS) * gain_vec + shift_vec


def softmax_rows(scores):
    highest = jnp.max(scores, -1, keepdims=True)
    exponent = jnp.exp(scores - highest)
    return exponent / jnp.sum(exponent, -1, keepdims=True)


def exact_gelu(values):
    return jax.nn.gelu(values, approximate=False)


def adam_update(weight, moment_one, moment_two, gradient, factor, decay_rate):
    clipped = gradient * factor
    new_first = BETA_ONE * moment_one + (1.0 - BETA_ONE) * clipped
    new_second = BETA_TWO * moment_two + (1.0 - BETA_TWO) * clipped * clipped
    direction = (
        new_first
        / (1.0 - BETA_ONE**STEP)
        / (jnp.sqrt(new_second / (1.0 - BETA_TWO**STEP)) + ADAM_EPS)
    )
    return (weight - LEARN_RATE * (direction + decay_rate * weight), new_first, new_second)


def offset_table():
    extent = 2 * GRID - 1
    place = jnp.arange(GRID)
    return (
        place[:, None, None] - place[None, :, None] + GRID - 1 == jnp.arange(extent)[None, None, :]
    ).astype(jnp.float32)


def bias_block(rel_local, axis_hot):
    heads_here = rel_local.shape[0]
    extent = 2 * GRID - 1
    inner = rel_local[:, : extent * extent].reshape(heads_here, extent, extent)
    across = jnp.einsum("hij,qsj->hiqs", inner, axis_hot, precision=HIGHEST)
    spread = jnp.einsum("hiqs,pri->hpqrs", across, axis_hot, precision=HIGHEST).reshape(
        heads_here, PATCH, PATCH
    )
    top_row = jnp.concatenate(
        [
            rel_local[:, NREL - 1][:, None, None],
            jnp.broadcast_to(rel_local[:, NREL - 3][:, None, None], (heads_here, 1, PATCH)),
        ],
        2,
    )
    lower_rows = jnp.concatenate(
        [jnp.broadcast_to(rel_local[:, NREL - 2][:, None, None], (heads_here, PATCH, 1)), spread], 2
    )
    return jnp.concatenate([top_row, lower_rows], 1)


def bias_grad(score_sums, axis_hot):
    heads_here = score_sums.shape[0]
    extent = 2 * GRID - 1
    inner = score_sums[:, 1:, 1:].reshape(heads_here, GRID, GRID, GRID, GRID)
    across = jnp.einsum("hpqrs,qsj->hprj", inner, axis_hot, precision=HIGHEST)
    folded = jnp.einsum("hprj,pri->hij", across, axis_hot, precision=HIGHEST).reshape(
        heads_here, extent * extent
    )
    extras = jnp.stack(
        [jnp.sum(score_sums[:, 0, 1:], 1), jnp.sum(score_sums[:, 1:, 0], 1), score_sums[:, 0, 0]], 1
    )
    return jnp.concatenate([folded, extras], 1)


def factor(ndp):
    half = ndp // 2
    inner = 1
    while inner * inner < half:
        inner *= 2
    return half // inner, inner


class Place:
    def __init__(self, outer, inner, members):
        index = lax.axis_index("dp")
        self.sizes = {"a": outer, "b": inner, "c": 2, "m": members}
        self.at = {
            "a": lax.div(index, 2 * inner),
            "b": lax.rem(lax.div(index, 2), inner),
            "c": lax.rem(index, 2),
            "m": lax.axis_index("mp"),
        }

    def shifted(self, axis, step):
        size = self.sizes[axis]
        return lax.rem(self.at[axis] + (step + size) % size, size)

    def device(self, axis, step):
        spot = dict(self.at)
        spot[axis] = self.shifted(axis, step)
        return ((spot["a"] * self.sizes["b"] + spot["b"]) * 2 + spot["c"], spot["m"])

    def enter(self):
        barrier = pltpu.get_barrier_semaphore()
        total = 0
        for axis, size in self.sizes.items():
            for step in range(1, size):
                pl.semaphore_signal(
                    barrier, inc=1, device_id=self.device(axis, step), device_id_type=MESH
                )
                total += 1
        pl.semaphore_wait(barrier, total)


def gather_kernel(outer, inner, members, groups, count, look, *refs):
    ins = refs[:count]
    outs = refs[count : 2 * count]
    send, recv, own = refs[2 * count :]
    place = Place(outer, inner, members)
    a, b, c, m = (place.at[axis] for axis in "abcm")
    place.enter()
    used = [0]

    def copies(piece, stage):
        i, first_row, rows, order = piece
        out = outs[i]
        width = ins[i].shape[1]
        span = pl.ds(first_row, rows)
        if stage == 0:
            axis, src = "m", ins[i].at[span]
            dst = out.at[a, b, c, span, pl.ds(pl.multiple_of(m * width, 128), width)]
        elif stage == 3:
            axis, src = "c", out.at[:, :, c, span]
            dst = src
        else:
            axis = order[stage - 1]
            if stage == 1:
                src = out.at[a, b, c, span]
            elif axis == "a":
                src = out.at[a, :, c, span]
            else:
                src = out.at[:, b, c, span]
            dst = src
        made = []
        for step in range(1, place.sizes[axis]):
            k = used[0]
            used[0] += 1
            made.append(
                pltpu.make_async_remote_copy(
                    src_ref=src,
                    dst_ref=dst,
                    send_sem=send.at[k],
                    recv_sem=recv.at[k],
                    device_id=place.device(axis, step),
                    device_id_type=MESH,
                )
            )
        return made

    flying = {}

    def start(group, stage):
        made = [copy for piece in groups[group] for copy in copies(piece, stage)]
        for copy in made:
            copy.start()
        flying[group, stage] = made

    total = len(groups)
    for group in range(min(look, total)):
        start(group, 0)
    local = []
    for i in range(count):
        width = ins[i].shape[1]
        mine = pl.ds(pl.multiple_of(m * width, 128), width)
        local.append(pltpu.make_async_copy(ins[i], outs[i].at[a, b, c, :, mine], own.at[i]))
    for copy in local:
        copy.start()
    for copy in local:
        copy.wait()
    for tick in range(total + 3):
        if tick + look < total:
            start(tick + look, 0)
        for stage in (2, 1, 0, 3):
            group = tick - stage
            if 0 <= group < total:
                for copy in flying[group, stage]:
                    copy.wait_recv()
                if stage < 3:
                    start(group, stage + 1)
    for made in flying.values():
        for copy in made:
            copy.wait_send()


def gather_blocks(blocks, ndp, members):
    outer, inner = factor(ndp)
    groups = []
    for i, block in enumerate(blocks):
        rows = block.shape[0]
        if rows % 32:
            groups.append([(i, 0, rows, "ab")])
        else:
            groups.append([(i, 0, rows // 2, "ab"), (i, rows // 2, rows // 2, "ba")])
    count = len(blocks)
    peers = (outer - 1) + (inner - 1) + 1 + (members - 1)
    sems = sum(len(group) for group in groups) * peers
    return pl.pallas_call(
        functools.partial(gather_kernel, outer, inner, members, groups, count, 2),
        out_shape=[
            jax.ShapeDtypeStruct((outer, inner, 2, x.shape[0], members * x.shape[1]), x.dtype)
            for x in blocks
        ],
        in_specs=[pl.BlockSpec(memory_space=pl.ANY)] * count,
        out_specs=[pl.BlockSpec(memory_space=pl.ANY)] * count,
        scratch_shapes=[
            pltpu.SemaphoreType.DMA((sems,)),
            pltpu.SemaphoreType.DMA((sems,)),
            pltpu.SemaphoreType.DMA((count,)),
        ],
        compiler_params=pltpu.CompilerParams(collective_id=0, has_side_effects=True),
        name="gather_blocks",
    )(*blocks)


class Channel:
    def __init__(self, place, axis, slots, total, send, recv, free):
        self.place, self.axis, self.slots, self.total = place, axis, slots, total
        self.send_sem, self.recv_sem, self.free = send, recv, free
        self.steps = range(1, place.sizes[axis])
        self.made = {}

    def before_fill(self, turn):
        if turn >= self.slots:
            for copy in self.made[turn - self.slots]:
                copy.wait_send()

    def send(self, turn, pairs):
        slot = turn % self.slots
        self.made[turn] = []
        for step, (src, dst) in zip(self.steps, pairs):
            if turn >= self.slots:
                pl.semaphore_wait(self.free.at[step - 1], 1)
            copy = pltpu.make_async_remote_copy(
                src_ref=src,
                dst_ref=dst,
                send_sem=self.send_sem.at[slot, step - 1],
                recv_sem=self.recv_sem.at[slot, step - 1],
                device_id=self.place.device(self.axis, step),
                device_id_type=MESH,
            )
            copy.start()
            self.made[turn].append(copy)

    def receive(self, turn):
        for copy in self.made[turn]:
            copy.wait_recv()

    def consumed(self, turn):
        if turn + self.slots < self.total:
            for step in self.steps:
                pl.semaphore_signal(
                    self.free.at[step - 1],
                    inc=1,
                    device_id=self.place.device(self.axis, -step),
                    device_id_type=MESH,
                )

    def drain(self):
        for turn in range(max(0, self.total - self.slots), self.total):
            for copy in self.made[turn]:
                copy.wait_send()


def reduce_kernel(outer, inner, members, rows, halves, groups, arrays, lags, *refs):
    refs = list(refs)

    def take(number):
        taken = refs[:number]
        del refs[:number]
        return taken

    (small_in,) = take(1)
    lefts = take(arrays)
    rights = take(arrays)
    outs = take(arrays)
    small_out, square_out = take(2)
    right_buf, right_sem = take(2)
    sent0, got0, own0 = take(3)
    sent1a, got1a, keep1a, sent1b, got1b, keep1b = take(6)
    sent2a, got2a, sent2b, got2b, keep2 = take(5)
    sent3, got3 = take(2)
    sems = [take(3) for _ in range(6)]
    small_bufs = take(4)
    square_bufs = take(4)
    tiny_send, tiny_recv = take(2)

    place = Place(outer, inner, members)
    a, b, c, m = (place.at[axis] for axis in "abcm")
    total = len(groups)
    top, low_rows = halves
    lag1, lag2, lag3, lag4 = lags
    slots = (2, lag2 - lag1, lag3 - lag2, lag4 - lag3)
    chan0 = Channel(place, "c", slots[0], total, *sems[0])
    chan1a = Channel(place, "a", slots[1], total, *sems[1])
    chan1b = Channel(place, "b", slots[1], total, *sems[2])
    chan2a = Channel(place, "b", slots[2], total, *sems[3])
    chan2b = Channel(place, "a", slots[2], total, *sems[4])
    chan3 = Channel(place, "m", slots[3], total, *sems[5])
    channels = [chan0, chan1a, chan2a, chan3]
    if low_rows:
        channels += [chan1b, chan2b]

    def each_member(body):
        def step(i, unused):
            body(i)
            return 0

        lax.fori_loop(0, members, step, 0)

    def fetch(turn):
        i, first, width = groups[turn]
        block = rights[i].shape[1] // members
        depth = rights[i].shape[0]
        return [
            pltpu.make_async_copy(
                rights[i].at[:, pl.ds(k * block + first, width)],
                right_buf.at[turn % 2, k, pl.ds(0, depth), pl.ds(0, width)],
                right_sem.at[turn % 2, k],
            )
            for k in range(members)
        ]

    def product(turn, half, k):
        i, first, width = groups[turn]
        depth = rights[i].shape[0]
        return jnp.dot(
            lefts[i][half],
            right_buf[turn % 2, k, pl.ds(0, depth), pl.ds(0, width)],
            preferred_element_type=jnp.float32,
        ).reshape(outer, inner, rows, width)

    def make(turn):
        i, first, width = groups[turn]
        cols = pl.ds(0, width)
        slot = turn % 2
        for copy in fetch(turn):
            copy.wait()
        if turn + 1 < total:
            for copy in fetch(turn + 1):
                copy.start()
        chan0.before_fill(turn)

        def fill(k):
            sent0[slot, k, :, :, :, cols] = product(turn, 1 - c, k).astype(jnp.bfloat16)

        each_member(fill)
        chan0.send(
            turn, [(sent0.at[slot, :, :, :, :, cols], got0.at[slot, :, :, :, :, cols])]
        )

        def fill_own(k):
            own0[slot, k, :, :, :, cols] = product(turn, c, k)

        each_member(fill_own)

    def stage_one(turn):
        i, first, width = groups[turn]
        cols = pl.ds(0, width)
        old, new = turn % 2, turn % slots[1]
        upper, lower = pl.ds(0, top), pl.ds(top, low_rows)
        chan1a.before_fill(turn)
        if low_rows:
            chan1b.before_fill(turn)
        chan0.receive(turn)

        def body(k):
            for step in range(outer):
                part = place.shifted("a", step)
                summed = own0[old, k, part, :, upper, cols] + got0[
                    old, k, part, :, upper, cols
                ].astype(jnp.float32)
                if step:
                    sent1a[new, step - 1, k, :, :, cols] = summed.astype(jnp.bfloat16)
                else:
                    keep1a[new, k, :, :, cols] = summed
            if low_rows:
                for step in range(inner):
                    part = place.shifted("b", step)
                    summed = own0[old, k, :, part, lower, cols] + got0[
                        old, k, :, part, lower, cols
                    ].astype(jnp.float32)
                    if step:
                        sent1b[new, step - 1, k, :, :, cols] = summed.astype(jnp.bfloat16)
                    else:
                        keep1b[new, k, :, :, cols] = summed

        each_member(body)
        chan0.consumed(turn)
        chan1a.send(
            turn,
            [
                (sent1a.at[new, j, :, :, :, cols], got1a.at[new, j, :, :, :, cols])
                for j in range(outer - 1)
            ],
        )
        if low_rows:
            chan1b.send(
                turn,
                [
                    (sent1b.at[new, j, :, :, :, cols], got1b.at[new, j, :, :, :, cols])
                    for j in range(inner - 1)
                ],
            )

    def stage_two(turn):
        i, first, width = groups[turn]
        cols = pl.ds(0, width)
        old, new = turn % slots[1], turn % slots[2]
        chan2a.before_fill(turn)
        if low_rows:
            chan2b.before_fill(turn)
        chan1a.receive(turn)
        if low_rows:
            chan1b.receive(turn)

        def body(k):
            for step in range(inner):
                part = place.shifted("b", step)
                summed = keep1a[old, k, part, :, cols]
                for j in range(outer - 1):
                    summed += got1a[old, j, k, part, :, cols].astype(jnp.float32)
                if step:
                    sent2a[new, step - 1, k, :, cols] = summed.astype(jnp.bfloat16)
                else:
                    keep2[new, k, pl.ds(0, top), cols] = summed
            if low_rows:
                for step in range(outer):
                    part = place.shifted("a", step)
                    summed = keep1b[old, k, part, :, cols]
                    for j in range(inner - 1):
                        summed += got1b[old, j, k, part, :, cols].astype(jnp.float32)
                    if step:
                        sent2b[new, step - 1, k, :, cols] = summed.astype(jnp.bfloat16)
                    else:
                        keep2[new, k, pl.ds(top, low_rows), cols] = summed

        each_member(body)
        chan1a.consumed(turn)
        if low_rows:
            chan1b.consumed(turn)
        chan2a.send(
            turn,
            [
                (sent2a.at[new, j, :, :, cols], got2a.at[new, j, :, :, cols])
                for j in range(inner - 1)
            ],
        )
        if low_rows:
            chan2b.send(
                turn,
                [
                    (sent2b.at[new, j, :, :, cols], got2b.at[new, j, :, :, cols])
                    for j in range(outer - 1)
                ],
            )

    def stage_three(turn):
        i, first, width = groups[turn]
        cols = pl.ds(0, width)
        old, new = turn % slots[2], turn % slots[3]
        chan3.before_fill(turn)
        chan2a.receive(turn)
        if low_rows:
            chan2b.receive(turn)

        def body(k):
            summed = keep2[old, k, pl.ds(0, top), cols]
            for j in range(inner - 1):
                summed += got2a[old, j, k, :, cols].astype(jnp.float32)
            sent3[new, k, pl.ds(0, top), cols] = summed
            if low_rows:
                summed = keep2[old, k, pl.ds(top, low_rows), cols]
                for j in range(outer - 1):
                    summed += got2b[old, j, k, :, cols].astype(jnp.float32)
                sent3[new, k, pl.ds(top, low_rows), cols] = summed

        each_member(body)
        chan2a.consumed(turn)
        if low_rows:
            chan2b.consumed(turn)
        chan3.send(
            turn,
            [
                (sent3.at[new, place.shifted("m", j + 1), :, cols], got3.at[new, j, :, cols])
                for j in range(members - 1)
            ],
        )

    def stage_four(turn):
        i, first, width = groups[turn]
        cols = pl.ds(0, width)
        old = turn % slots[3]
        chan3.receive(turn)
        summed = sent3[old, m, :, cols]
        for j in range(members - 1):
            summed += got3[old, j, :, cols]
        outs[i][:, pl.ds(first, width)] = summed
        chan3.consumed(turn)

    tiny_used = [0]
    tiny_made = []

    def spread(buf, axis):
        made = []
        entry = buf.at[place.at[axis]]
        for step in range(1, place.sizes[axis]):
            k = tiny_used[0]
            tiny_used[0] += 1
            copy = pltpu.make_async_remote_copy(
                src_ref=entry,
                dst_ref=entry,
                send_sem=tiny_send.at[k],
                recv_sem=tiny_recv.at[k],
                device_id=place.device(axis, step),
                device_id_type=MESH,
            )
            copy.start()
            made.append(copy)
        tiny_made.extend(made)
        return made

    def sum_entries(buf, made):
        for copy in made:
            copy.wait_recv()
        summed = buf[0]
        for k in range(1, buf.shape[0]):
            summed += buf[k]
        return summed

    place.enter()
    for copy in fetch(0):
        copy.start()
    small_made = [None] * 4
    for tick in range(total + lag4):
        if lag4 <= tick:
            stage_four(tick - lag4)
        if 0 <= tick - lag3 < total:
            stage_three(tick - lag3)
        if 0 <= tick - lag2 < total:
            stage_two(tick - lag2)
        if 0 <= tick - lag1 < total:
            stage_one(tick - lag1)
        if tick < total:
            make(tick)
        if tick in (1, 3, 5, 7, 9):
            hop = (tick - 1) // 2
            value = small_in[...] if hop == 0 else sum_entries(small_bufs[hop - 1], small_made[hop - 1])
            if hop == 4:
                small_out[...] = value
            else:
                axis = "cabm"[hop]
                small_bufs[hop][place.at[axis]] = value
                small_made[hop] = spread(small_bufs[hop], axis)
    for channel in channels:
        channel.drain()
    value = jnp.zeros((8, 128), jnp.float32)
    for i in range(arrays):
        block = outs[i][...]
        value += jnp.sum((block * block).reshape(-1, 8, 128), 0) if block.shape[1] == 128 else sum_tiles(block)
    for hop, axis in enumerate("cabm"):
        square_bufs[hop][place.at[axis]] = value
        value = sum_entries(square_bufs[hop], spread(square_bufs[hop], axis))
    square_out[...] = value
    for copy in tiny_made:
        copy.wait_send()


def sum_tiles(block):
    squares = block * block
    folded = squares[:8]
    for first in range(8, block.shape[0], 8):
        folded += squares[first : first + 8]
    total = folded[:, :128]
    for first in range(128, block.shape[1], 128):
        total += folded[:, first : first + 128]
    return total


def reduce_products(pairs, small, ndp, members):
    outer, inner = factor(ndp)
    per_device = pairs[0][0].shape[1] // ndp
    rows = -(-per_device // 16) * 16
    both = outer * inner
    wide = both * rows <= 400
    halves = (rows // 2, rows // 2) if rows % 32 == 0 else (rows, 0)
    top, low_rows = halves
    low_shape = max(low_rows, 16)
    lags = (1, 3, 5, 7)
    slots = (2, 2, 2, 2)
    lefts, rights, groups, outs = [], [], [], []
    for i, (x, y) in enumerate(pairs):
        depth = x.shape[0]
        turned = x.T.reshape(both, 2, per_device, depth)
        turned = jnp.pad(turned, ((0, 0), (0, 0), (0, rows - per_device), (0, 0)))
        lefts.append(turned.transpose(1, 0, 2, 3).reshape(2, both * rows, depth))
        rights.append(y)
        block = y.shape[1] // members
        width = (512 if block % 512 == 0 else 384) if wide else 256
        groups += [(i, first, width) for first in range(0, block, width)]
        outs.append(jax.ShapeDtypeStruct((rows, block), jnp.float32))
    most = max(width for _, _, width in groups)
    deepest = max(y.shape[0] for y in rights)
    count = len(pairs)
    small_shape = small.shape
    bf, f4 = jnp.bfloat16, jnp.float32
    mem = pltpu.VMEM
    scratch = [
        mem((2, members, deepest, most), bf),
        pltpu.SemaphoreType.DMA((2, members)),
        mem((slots[0], members, outer, inner, rows, most), bf),
        mem((slots[0], members, outer, inner, rows, most), bf),
        mem((2, members, outer, inner, rows, most), f4),
        mem((slots[1], outer - 1, members, inner, top, most), bf),
        mem((slots[1], outer - 1, members, inner, top, most), bf),
        mem((slots[1], members, inner, top, most), f4),
        mem((slots[1], inner - 1, members, outer, low_shape, most), bf),
        mem((slots[1], inner - 1, members, outer, low_shape, most), bf),
        mem((slots[1], members, outer, low_shape, most), f4),
        mem((slots[2], inner - 1, members, top, most), bf),
        mem((slots[2], inner - 1, members, top, most), bf),
        mem((slots[2], outer - 1, members, low_shape, most), bf),
        mem((slots[2], outer - 1, members, low_shape, most), bf),
        mem((slots[2], members, rows, most), f4),
        mem((slots[3], members, rows, most), f4),
        mem((slots[3], members - 1, rows, most), f4),
    ]
    for depth, size in zip((0, 1, 1, 2, 2, 3), (2, outer, inner, inner, outer, members)):
        scratch += [
            pltpu.SemaphoreType.DMA((slots[depth], size - 1)),
            pltpu.SemaphoreType.DMA((slots[depth], size - 1)),
            pltpu.SemaphoreType.REGULAR((size - 1,)),
        ]
    sizes = (2, outer, inner, members)
    scratch += [mem((size,) + small_shape, f4) for size in sizes]
    scratch += [mem((size, 8, 128), f4) for size in sizes]
    tiny = 2 * sum(size - 1 for size in sizes)
    scratch += [pltpu.SemaphoreType.DMA((tiny,)), pltpu.SemaphoreType.DMA((tiny,))]
    vmem = pl.BlockSpec(memory_space=pltpu.VMEM)
    results = pl.pallas_call(
        functools.partial(
            reduce_kernel, outer, inner, members, rows, halves, groups, count, lags
        ),
        out_shape=outs
        + [jax.ShapeDtypeStruct(small_shape, f4), jax.ShapeDtypeStruct((8, 128), f4)],
        in_specs=[vmem] * (1 + count) + [pl.BlockSpec(memory_space=pl.ANY)] * count,
        out_specs=[vmem] * (count + 2),
        scratch_shapes=scratch,
        compiler_params=pltpu.CompilerParams(
            collective_id=1, has_side_effects=True, vmem_limit_bytes=62 * 2**20
        ),
        name="reduce_products",
    )(small, *lefts, *rights)
    return [block[:per_device] for block in results[:count]], results[count], results[count + 1]


def local(members, ndp, *args):
    (
        qkv_weight, qkv_first, qkv_second,
        out_weight, out_first, out_second,
        up_weight, up_first, up_second,
        down_weight, down_first, down_second,
        code_table, table_first, table_second,
        small_params, small_first, small_second,
        patch_codes, masked_pos, masked_count,
    ) = args
    bf, f4 = jnp.bfloat16, jnp.float32
    member = lax.axis_index("mp")
    images = patch_codes.shape[0] // members
    rows_all = images * SEQ
    depth = -(-rows_all // 16) * 16
    heads_part = H // members
    width_part = D // members
    score_scale = DH ** (-0.5)
    axis_hot = offset_table()
    vectors, fc_bias, rel_tables, special = unpack_small(small_params)

    blocks = []
    count_here = jnp.full((8, 128), jnp.sum(masked_count).astype(f4))
    for l in range(LAYERS):
        blocks.append(
            jnp.concatenate(
                [qkv_weight[l, 0], qkv_weight[l, 1], qkv_weight[l, 2], out_weight[l].T], 1
            ).astype(bf)
        )
        blocks.append(up_weight[l].astype(bf))
        blocks.append(down_weight[l].T.astype(bf))
    blocks = [blocks[0], code_table.T.astype(bf)] + blocks[1:] + [count_here]
    gathered = list(gather_blocks(blocks, ndp, members))
    counts_all = gathered.pop()
    mats = [g.reshape(D, g.shape[-1]) for g in gathered]
    table = mats.pop(1)
    layer_mats = [mats[3 * l : 3 * l + 3] for l in range(LAYERS)]
    count_total = jnp.sum(counts_all.reshape(ndp, 8, members * 128)[:, 0, 0])
    inverse_total = jnp.ones((), f4) / count_total

    def mine(values):
        return lax.dynamic_slice_in_dim(values, member * images, images, 0)

    image_codes = mine(patch_codes)
    masked_spots = mine(masked_pos)
    counts = mine(masked_count)
    valid_slots = jnp.arange(MAXM)[None, :] < counts[:, None]
    hidden_patch = jnp.any(
        (masked_spots[:, :, None] == jnp.arange(PATCH)[None, None, :]) & valid_slots[:, :, None], 1
    )
    masked_rows = jnp.concatenate([jnp.zeros((images, 1), jnp.bool_), hidden_patch], 1).reshape(-1)
    cls_rows = jnp.arange(rows_all) % SEQ == 0
    seen_rows = jnp.logical_not(masked_rows | cls_rows)
    row_codes = jnp.concatenate([jnp.zeros((images, 1), jnp.int32), image_codes], 1).reshape(-1)
    code_hot = (seen_rows[:, None] & (row_codes[:, None] == jnp.arange(V)[None, :])).astype(bf)
    pick_hot = (masked_spots[:, :, None] + 1 == jnp.arange(SEQ)[None, None, :]).astype(f4)
    targets = jnp.take_along_axis(image_codes, masked_spots, 1).reshape(-1)
    valid_float = valid_slots.reshape(-1).astype(f4)
    row_weight = valid_float * inverse_total

    def by_rows(x, w):
        return lax.dot_general(x, w, (((1,), (1,)), ((), ())), preferred_element_type=f4)

    def dot(x, w):
        return jnp.dot(x, w, preferred_element_type=f4)

    def split_heads(values):
        return values.reshape(images, SEQ, H, DH)

    def out_part(attn_mat):
        return attn_mat.reshape(D, members, 4 * width_part)[:, :, 3 * width_part :].reshape(D, D)

    embedded = by_rows(code_hot, table)
    fallback = jnp.where(cls_rows[:, None], special[0], special[1])
    x = jnp.where(seen_rows[:, None], embedded, fallback)
    caches = []
    for l in range(LAYERS):
        attn_mat, up_mat, down_mat = layer_mats[l]
        vec = vectors[l]
        attn_in = layer_norm(x, vec[0], vec[1]).astype(bf)
        projected = dot(attn_in, attn_mat).reshape(rows_all, members, 4, width_part)
        query_rows = (projected[:, :, 0].reshape(rows_all, D) + vec[2]).astype(bf)
        key_rows = projected[:, :, 1].reshape(rows_all, D).astype(bf)
        value_rows = (projected[:, :, 2].reshape(rows_all, D) + vec[3]).astype(bf)
        rel_bias = bias_block(rel_tables[l], axis_hot)
        raw_scores = jnp.einsum(
            "bqhd,bkhd->bhqk", split_heads(query_rows), split_heads(key_rows),
            preferred_element_type=f4,
        )
        attn_probs = softmax_rows(raw_scores * score_scale + rel_bias[None])
        mixed = (
            jnp.einsum(
                "bhqk,bkhd->bqhd", attn_probs.astype(bf), split_heads(value_rows),
                preferred_element_type=f4,
            )
            .reshape(rows_all, D)
            .astype(bf)
        )
        out_mat = out_part(attn_mat)
        attn_out = by_rows(mixed, out_mat) + vec[4]
        x_mid = x + vec[5] * attn_out
        mlp_in = layer_norm(x_mid, vec[6], vec[7]).astype(bf)
        pre_act = dot(mlp_in, up_mat) + fc_bias[l]
        activated = exact_gelu(pre_act).astype(bf)
        mlp_out = by_rows(activated, down_mat) + vec[8]
        caches.append(
            (x, attn_in, query_rows, key_rows, value_rows, attn_probs, mixed, out_mat, attn_out,
             x_mid, mlp_in, pre_act, activated, mlp_out)
        )
        x = x_mid + vec[9] * mlp_out

    last_normed = layer_norm(x, special[2], special[3]).astype(bf)
    picked = (
        jnp.einsum(
            "bst,btd->bsd", pick_hot.astype(bf), last_normed.reshape(images, SEQ, D),
            preferred_element_type=f4,
        )
        .astype(bf)
        .reshape(images * MAXM, D)
    )
    logits = dot(picked, table)
    target_hits = jnp.arange(V)[None, :] == targets[:, None]
    target_logit = jnp.sum(jnp.where(target_hits, logits, 0.0), 1)
    highest = jnp.max(logits, 1)
    exp_sums = jnp.sum(jnp.exp(logits - highest[:, None]), 1)
    log_total = highest + jnp.log(exp_sums)
    loss_part = jnp.sum((log_total - target_logit) * valid_float)
    d_logits = (
        (jnp.exp(logits - log_total[:, None]) - target_hits.astype(f4)) * row_weight[:, None]
    ).astype(bf)
    d_picked = by_rows(d_logits, table)
    d_normed = jnp.einsum(
        "bst,bsd->btd", pick_hot, d_picked.reshape(images, MAXM, D), precision=HIGHEST
    ).reshape(rows_all, D)
    unused, pullback = jax.vjp(layer_norm, x, special[2], special[3])
    upstream, d_gain, d_shift = pullback(d_normed)

    def padded(values):
        return jnp.pad(values, ((0, depth - rows_all), (0, 0)))

    pairs = [None] * LAYERS
    vec_grads, fc_grads, rel_grads = [None] * LAYERS, [None] * LAYERS, [None] * LAYERS
    for l in reversed(range(LAYERS)):
        attn_mat, up_mat, down_mat = layer_mats[l]
        (x_in, attn_in, query_rows, key_rows, value_rows, attn_probs, mixed, out_mat, attn_out,
         x_mid, mlp_in, pre_act, activated, mlp_out) = caches[l]
        vec = vectors[l]
        g_mlp = (vec[9] * upstream).astype(bf)
        d_gamma2 = jnp.sum(upstream * mlp_out, 0)
        d_down_bias = jnp.sum(g_mlp.astype(f4), 0)
        d_act = dot(g_mlp, down_mat)
        unused, pullback = jax.vjp(exact_gelu, pre_act)
        d_pre = pullback(d_act)[0].astype(bf)
        fc_grads[l] = jnp.sum(d_pre.astype(f4), 0)
        d_norm2 = by_rows(d_pre, up_mat)
        unused, pullback = jax.vjp(layer_norm, x_mid, vec[6], vec[7])
        d_mid, d_gain2, d_shift2 = pullback(d_norm2)
        d_mid = d_mid + upstream
        g_attn = (vec[5] * d_mid).astype(bf)
        d_gamma1 = jnp.sum(d_mid * attn_out, 0)
        d_out_bias = jnp.sum(g_attn.astype(f4), 0)
        d_mixed = split_heads(dot(g_attn, out_mat).astype(bf))
        d_probs = jnp.einsum(
            "bqhd,bkhd->bhqk", d_mixed, split_heads(value_rows), preferred_element_type=f4
        )
        d_value = jnp.einsum(
            "bhqk,bqhd->bkhd", attn_probs.astype(bf), d_mixed, preferred_element_type=f4
        ).astype(bf)
        d_scores = (
            attn_probs * (d_probs - jnp.sum(attn_probs * d_probs, -1, keepdims=True))
        ).astype(bf)
        d_query = (
            jnp.einsum(
                "bhqk,bkhd->bqhd", d_scores, split_heads(key_rows), preferred_element_type=f4
            )
            * score_scale
        ).astype(bf)
        d_key = (
            jnp.einsum(
                "bhqk,bqhd->bkhd", d_scores, split_heads(query_rows), preferred_element_type=f4
            )
            * score_scale
        ).astype(bf)
        rel_grads[l] = bias_grad(jnp.sum(d_scores.astype(f4), 0), axis_hot)

        def parts(values):
            return values.reshape(rows_all, members, 1, width_part)

        d_cat = jnp.concatenate(
            [parts(d_query), parts(d_key), parts(d_value), jnp.zeros_like(parts(d_value))], 2
        ).reshape(rows_all, 4 * D)
        mixed_cat = jnp.pad(parts(mixed), ((0, 0), (0, 0), (3, 0), (0, 0))).reshape(rows_all, 4 * D)
        d_norm1 = by_rows(d_cat, attn_mat)
        unused, pullback = jax.vjp(layer_norm, x_in, vec[0], vec[1])
        d_input, d_gain1, d_shift1 = pullback(d_norm1)
        vec_grads[l] = jnp.stack(
            [
                d_gain1, d_shift1,
                jnp.sum(d_query.reshape(rows_all, D).astype(f4), 0),
                jnp.sum(d_value.reshape(rows_all, D).astype(f4), 0),
                d_out_bias, d_gamma1, d_gain2, d_shift2, d_down_bias, d_gamma2,
            ]
        )
        pairs[l] = [
            (
                jnp.concatenate([padded(attn_in), padded(g_attn)], 0),
                jnp.concatenate([padded(d_cat), padded(mixed_cat)], 0),
            ),
            (padded(mlp_in), padded(d_pre)),
            (padded(g_mlp), padded(activated)),
        ]
        upstream = d_input + d_mid
    d_cls = jnp.sum(jnp.where(cls_rows[:, None], upstream, 0.0), 0)
    d_mask = jnp.sum(jnp.where(masked_rows[:, None], upstream, 0.0), 0)
    seen_grad = jnp.where(seen_rows[:, None], upstream, 0.0).astype(bf)
    table_depth = images * MAXM + rows_all
    table_pad = ((0, -table_depth % 16), (0, 0))
    table_pair = (
        jnp.pad(jnp.concatenate([picked, seen_grad], 0), table_pad),
        jnp.pad(jnp.concatenate([d_logits, code_hot], 0), table_pad),
    )
    small_grad = pack_small(
        jnp.stack(vec_grads), jnp.stack(fc_grads), jnp.stack(rel_grads),
        jnp.stack([d_cls, d_mask, d_gain, d_shift]),
    )
    small_size = small_grad.shape[0]
    packed = jnp.concatenate([small_grad, loss_part[None]])
    packed = jnp.pad(packed, (0, -packed.shape[0] % 1024)).reshape(-1, 128)

    all_pairs = [table_pair] + [pair for l in reversed(range(LAYERS)) for pair in pairs[l]]
    grads, small_sum, squares = reduce_products(all_pairs, packed, ndp, members)
    grad_table = grads[0].T
    by_layer = [grads[1 + 3 * (LAYERS - 1 - l) :][:3] for l in range(LAYERS)]
    grad_qkv = jnp.stack(
        [
            jnp.stack([g[0][:, j * width_part : (j + 1) * width_part] for j in range(3)])
            for g in by_layer
        ]
    )
    grad_out = jnp.stack([g[0][:, 3 * width_part :].T for g in by_layer])
    grad_up = jnp.stack([g[1] for g in by_layer])
    grad_down = jnp.stack([g[2].T for g in by_layer])
    small_sum = small_sum.reshape(-1)
    grad_small = small_sum[:small_size]
    loss_total = small_sum[small_size]
    grad_norm = jnp.sqrt(jnp.sum(squares) + jnp.sum(grad_small * grad_small))
    factor_clip = jnp.minimum(1.0, CLIP_NORM / (grad_norm + 1e-06))
    results = ()
    for weight, one, two, grad, decay in (
        (qkv_weight, qkv_first, qkv_second, grad_qkv, WEIGHT_DECAY),
        (out_weight, out_first, out_second, grad_out, WEIGHT_DECAY),
        (up_weight, up_first, up_second, grad_up, WEIGHT_DECAY),
        (down_weight, down_first, down_second, grad_down, WEIGHT_DECAY),
        (code_table, table_first, table_second, grad_table, WEIGHT_DECAY),
        (small_params, small_first, small_second, grad_small, 0.0),
    ):
        results += adam_update(weight, one, two, grad, factor_clip, decay)
    return results + (loss_total, count_total, grad_norm)


def solution(mesh):
    in_specs = (
        P(None, None, "dp", "mp"),
        P(None, None, "dp", "mp"),
        P(None, None, "dp", "mp"),
        P(None, "mp", "dp"),
        P(None, "mp", "dp"),
        P(None, "mp", "dp"),
        P(None, "dp", "mp"),
        P(None, "dp", "mp"),
        P(None, "dp", "mp"),
        P(None, "mp", "dp"),
        P(None, "mp", "dp"),
        P(None, "mp", "dp"),
        P("mp", "dp"),
        P("mp", "dp"),
        P("mp", "dp"),
        P(),
        P(),
        P(),
        P("dp", None),
        P("dp", None),
        P("dp"),
    )
    out_specs = (
        P(None, None, "dp", "mp"),
        P(None, None, "dp", "mp"),
        P(None, None, "dp", "mp"),
        P(None, "mp", "dp"),
        P(None, "mp", "dp"),
        P(None, "mp", "dp"),
        P(None, "dp", "mp"),
        P(None, "dp", "mp"),
        P(None, "dp", "mp"),
        P(None, "mp", "dp"),
        P(None, "mp", "dp"),
        P(None, "mp", "dp"),
        P("mp", "dp"),
        P("mp", "dp"),
        P("mp", "dp"),
        P(),
        P(),
        P(),
        P(),
        P(),
        P(),
    )
    body = functools.partial(local, mesh.shape["mp"], mesh.shape["dp"])
    return jax.shard_map(body, mesh=mesh, in_specs=in_specs, out_specs=out_specs, check_vma=False)
```

```python
import functools

import jax
import jax.numpy as jnp
from jax import lax
from jax.experimental import pallas as pl
from jax.experimental.pallas import tpu as pltpu
from jax.sharding import PartitionSpec as P

D = 768
H = 12
DH = 64
FF = 3072
V = 8192
GRID = 14
LAYERS = 2
MAXM = 75
STEP = 10
SEQ = 197
PATCH = 196
NREL = 732


MESH = pl.DeviceIdType.MESH
NORM_EPS = 1e-06
CLIP_NORM = 0.02
LEARN_RATE = 0.03
BETA_ONE = 0.9
BETA_TWO = 0.98
ADAM_EPS = 1e-08
WEIGHT_DECAY = 0.05


def unpack_small(packed):
    first_end = LAYERS * 10 * D
    second_end = first_end + LAYERS * FF
    third_end = second_end + LAYERS * H * NREL
    vectors = packed[:first_end].reshape(LAYERS, 10, D)
    fc_bias = packed[first_end:second_end].reshape(LAYERS, FF)
    rel_tables = packed[second_end:third_end].reshape(LAYERS, H, NREL)
    special = packed[third_end:].reshape(4, D)
    return (vectors, fc_bias, rel_tables, special)


def pack_small(vectors, fc_bias, rel_tables, special):
    return jnp.concatenate(
        [vectors.reshape(-1), fc_bias.reshape(-1), rel_tables.reshape(-1), special.reshape(-1)]
    )


def adam_update(weight, moment_one, moment_two, gradient, factor, decay_rate):
    clipped = gradient * factor
    new_first = BETA_ONE * moment_one + (1.0 - BETA_ONE) * clipped
    new_second = BETA_TWO * moment_two + (1.0 - BETA_TWO) * clipped * clipped
    direction = (
        new_first
        / (1.0 - BETA_ONE**STEP)
        / (jnp.sqrt(new_second / (1.0 - BETA_TWO**STEP)) + ADAM_EPS)
    )
    return (weight - LEARN_RATE * (direction + decay_rate * weight), new_first, new_second)


IMG = 208
TILE = 128
REL_LANES = 768
KEY_LANES = 384


def dot_nn(x, w):
    return lax.dot_general(x, w, (((1,), (0,)), ((), ())), preferred_element_type=jnp.float32)


def dot_nt(x, w):
    return lax.dot_general(x, w, (((1,), (1,)), ((), ())), preferred_element_type=jnp.float32)


def dot_tn(x, w):
    return lax.dot_general(x, w, (((0,), (0,)), ((), ())), preferred_element_type=jnp.float32)


def three_parts(values):
    high = values.astype(jnp.bfloat16)
    rest = values - high.astype(jnp.float32)
    middle = rest.astype(jnp.bfloat16)
    low = (rest - middle.astype(jnp.float32)).astype(jnp.bfloat16)
    return high, middle, low


def exact_nn(values, hot):
    return sum(dot_nn(part, hot) for part in three_parts(values))


def exact_left(hot, values):
    return sum(dot_nn(hot, part) for part in three_parts(values))


def col_sum(values):
    return jnp.sum(values, 0, keepdims=True)


def norm_parts(values):
    average = jnp.mean(values, -1, keepdims=True)
    centred = values - average
    variance = jnp.mean(centred * centred, -1, keepdims=True)
    scale = lax.rsqrt(variance + NORM_EPS)
    return centred * scale, scale


def norm_backward(upstream, values, gain):
    unit, scale = norm_parts(values)
    d_gain = col_sum(upstream * unit)
    d_shift = col_sum(upstream)
    d_unit = upstream * gain
    mean_one = jnp.mean(d_unit, -1, keepdims=True)
    mean_two = jnp.mean(d_unit * unit, -1, keepdims=True)
    return scale * (d_unit - mean_one - unit * mean_two), d_gain, d_shift


def iota(shape, axis):
    return lax.broadcasted_iota(jnp.int32, shape, axis)


def bias_kernel(rel_ref, extra_ref, out_ref, wide_ref):
    extent = 2 * GRID - 1
    line = jnp.broadcast_to(rel_ref[0], (16, REL_LANES))
    line = pltpu.roll(line, 0, 1, stride=1, stride_axis=0)
    for p in range(GRID):
        first = (GRID - 1 - p) * extent + GRID - 1
        turned = pltpu.roll(line, REL_LANES - first, 1)
        wide_ref[pl.ds(16 * p, 16), :] = turned[:, :KEY_LANES]
    lane = iota((KEY_LANES, IMG), 0)
    key = iota((KEY_LANES, IMG), 1) - 1
    place = lax.div(key, GRID) * extent + lax.rem(key, GRID)
    columns = ((lane == place) & (key >= 0) & (key < PATCH)).astype(jnp.bfloat16)
    row = iota((IMG, 16 * GRID), 0) - 1
    spot = iota((IMG, 16 * GRID), 1)
    place = lax.div(row, GRID) * 16 + lax.rem(row, GRID)
    rows = ((spot == place) & (row >= 0) & (row < PATCH)).astype(jnp.bfloat16)
    inner = exact_left(rows, exact_nn(wide_ref[...], columns))
    query = iota((IMG, IMG), 0)
    key = iota((IMG, IMG), 1)
    extra = extra_ref[0]
    inner = jnp.where(query == 0, extra[:, 0:1], inner)
    inner = jnp.where(key == 0, jnp.where(query == 0, extra[:, 2:3], extra[:, 1:2]), inner)
    out_ref[0] = jnp.where(key < SEQ, inner, -1e30)


def rel_biases(rel_tables):
    number = LAYERS * H
    flat = rel_tables.reshape(number, 1, NREL)
    reverse = jnp.pad(flat[:, :, NREL - 4 :: -1], ((0, 0), (0, 0), (0, REL_LANES - NREL + 3)))
    extras = jnp.pad(flat[:, :, NREL - 3 :], ((0, 0), (0, 0), (0, TILE - 3)))
    return pl.pallas_call(
        bias_kernel,
        grid=(number,),
        in_specs=[
            pl.BlockSpec((1, 1, REL_LANES), lambda i: (i, 0, 0)),
            pl.BlockSpec((1, 1, TILE), lambda i: (i, 0, 0)),
        ],
        out_specs=pl.BlockSpec((1, IMG, IMG), lambda i: (i, 0, 0)),
        out_shape=jax.ShapeDtypeStruct((number, IMG, IMG), jnp.float32),
        scratch_shapes=[pltpu.VMEM((16 * GRID, KEY_LANES), jnp.float32)],
        name="rel_biases",
    )(reverse, extras)


def rel_grad_kernel(sums_ref, rel_ref, extra_ref):
    extent = 2 * GRID - 1
    sums = sums_ref[0]
    column = iota((IMG, KEY_LANES), 0) - 1
    lane = iota((IMG, KEY_LANES), 1)
    place = lax.div(column, GRID) * extent + lax.rem(column, GRID)
    columns = ((lane == place) & (column >= 0) & (column < PATCH)).astype(jnp.bfloat16)
    spot = iota((16 * GRID, IMG), 0)
    row = iota((16 * GRID, IMG), 1) - 1
    place = lax.div(row, GRID) * 16 + GRID - 1 - lax.rem(row, GRID)
    rows = ((spot == place) & (row >= 0) & (row < PATCH)).astype(jnp.bfloat16)
    wide = exact_nn(exact_left(rows, sums), columns)
    wide = jnp.concatenate([wide, jnp.zeros((16 * GRID, REL_LANES - KEY_LANES), jnp.float32)], 1)
    total = jnp.zeros((16, REL_LANES), jnp.float32)
    for p in range(GRID):
        first = (GRID - 1 - p) * extent
        total += pltpu.roll(wide[16 * p : 16 * p + 16], first, 1) if first else wide[16 * p : 16 * p + 16]
    rel_ref[0] = col_sum(pltpu.roll(total, 0, 1, stride=1, stride_axis=0))
    query = iota((IMG, IMG), 0)
    key = iota((IMG, IMG), 1)
    lanes = iota((1, TILE), 1)
    result = jnp.zeros((1, TILE), jnp.float32)
    for k, mask in enumerate(
        ((query == 0) & (key > 0), (query > 0) & (key == 0), (query == 0) & (key == 0))
    ):
        amount = jnp.sum(col_sum(jnp.where(mask, sums, 0.0)), 1, keepdims=True)
        result = jnp.where(lanes == k, amount, result)
    extra_ref[0] = result


def rel_grads(score_sums):
    number = LAYERS * H
    rel, extra = pl.pallas_call(
        rel_grad_kernel,
        grid=(number,),
        in_specs=[pl.BlockSpec((1, IMG, IMG), lambda i: (i, 0, 0))],
        out_specs=[
            pl.BlockSpec((1, 1, REL_LANES), lambda i: (i, 0, 0)),
            pl.BlockSpec((1, 1, TILE), lambda i: (i, 0, 0)),
        ],
        out_shape=[
            jax.ShapeDtypeStruct((number, 1, REL_LANES), jnp.float32),
            jax.ShapeDtypeStruct((number, 1, TILE), jnp.float32),
        ],
        name="rel_grads",
    )(score_sums)
    inner = rel[:, 0, NREL - 4 :: -1]
    return jnp.concatenate([inner, extra[:, 0, :3]], 1).reshape(LAYERS, H, NREL)


def head_views(k):
    return ((0, 1, 2, 1, 0, 0), (0, 1, 2, 1, 1, 1), (3, 4, 3, 0, 0, 1))[k]


def half_mask(rows, half):
    return (iota((rows, TILE), 1) < TILE // 2) == (half == 0)


def keep_half(values, half):
    return jnp.where(half_mask(values.shape[0], half), values, jnp.zeros_like(values))


def tile_of(ref, member, image, tile):
    return ref[member, pl.ds(image * IMG, IMG), pl.ds(tile * TILE, TILE)]


def head_probs(proj_ref, rel_ref, member, image, k):
    qt, kt, vt, ot, qk_half, vo_half = head_views(k)
    query = keep_half(tile_of(proj_ref, member, image, qt), qk_half)
    key = tile_of(proj_ref, member, image, kt)
    scores = dot_nt(query, key) * (DH ** (-0.5)) + rel_ref[3 * member + k]
    exponent = jnp.exp(scores - jnp.max(scores, -1, keepdims=True))
    return exponent / jnp.sum(exponent, -1, keepdims=True), query, key


def member_cols(member, first, width):
    return pl.ds(pl.multiple_of(member * (6 * TILE) + first * TILE, TILE), width * TILE)


def loop(number, body):
    def step(i, unused):
        body(i)
        return 0

    lax.fori_loop(0, number, step, 0)


def load(src, dst, sem):
    copy = pltpu.make_async_copy(src, dst, sem)
    copy.start()
    return copy


def embed_kernel(members, images, codes_ref, kind_ref, special_ref, table_hbm, x_ref, table_buf, sems):
    chunk = table_buf.shape[2]
    number = table_hbm.shape[1] // chunk
    for j in range(2):
        load(table_hbm.at[:, pl.ds(j * chunk, chunk)], table_buf.at[j], sems.at[j])
    x_ref[...] = jnp.zeros_like(x_ref)

    def body(j):
        slot = lax.rem(j, 2)
        src = table_hbm.at[:, pl.ds(pl.multiple_of(j * chunk, TILE), chunk)]
        pltpu.make_async_copy(src, table_buf.at[slot], sems.at[slot]).wait()
        hot = (codes_ref[...] == iota((codes_ref.shape[0], chunk), 1) + j * chunk).astype(
            jnp.bfloat16
        )
        x_ref[...] += dot_nt(hot, table_buf[slot])

        @pl.when(j + 2 < number)
        def _():
            src = table_hbm.at[:, pl.ds(pl.multiple_of((j + 2) * chunk, TILE), chunk)]
            load(src, table_buf.at[slot], sems.at[slot])

    loop(number, body)
    kind = kind_ref[...]
    fallback = jnp.where(kind == 1, special_ref[0:1, :], special_ref[1:2, :])
    x_ref[...] = jnp.where(kind == 0, x_ref[...], fallback)


def forward_kernel(
    members, images, x_ref, vec_ref, fc_ref, proj_bias_ref, rel_ref, attn_hbm, up_hbm, down_hbm,
    next_ref, proj_ref, mixed_ref, attn_out_ref, mid_ref, mlp_in_ref, pre_ref, act_ref, mlp_ref,
    attn_buf, up_buf, down_buf, sems,
):
    copies = [
        load(src, dst, sems.at[i])
        for i, (src, dst) in enumerate(
            ((attn_hbm, attn_buf), (up_hbm, up_buf), (down_hbm, down_buf))
        )
    ]
    unit, unused = norm_parts(x_ref[...])
    attn_in = (unit * vec_ref[0:1, :] + vec_ref[1:2, :]).astype(jnp.bfloat16)
    copies[0].wait()
    attn_out_ref[...] = jnp.broadcast_to(vec_ref[4:5, :], attn_out_ref.shape)

    def body(m):
        cols = member_cols(m, 0, 5)
        proj_ref[m] = (dot_nn(attn_in, attn_buf[:, cols]) + proj_bias_ref[:, cols]).astype(
            jnp.bfloat16
        )
        for image in range(images):
            outs = []
            for k in range(3):
                probs, unused, unused = head_probs(proj_ref, rel_ref, m, image, k)
                value = tile_of(proj_ref, m, image, head_views(k)[2])
                outs.append(dot_nn(probs.astype(jnp.bfloat16), value))
            rows = pl.ds(image * IMG, IMG)
            mixed_ref[m, rows, pl.ds(0, TILE)] = keep_half(outs[2], 1).astype(jnp.bfloat16)
            mixed_ref[m, rows, pl.ds(TILE, TILE)] = jnp.where(
                half_mask(IMG, 0), outs[0], outs[1]
            ).astype(jnp.bfloat16)
        attn_out_ref[...] += dot_nt(mixed_ref[m], attn_buf[:, member_cols(m, 4, 2)])

    loop(members, body)
    mid = x_ref[...] + vec_ref[5:6, :] * attn_out_ref[...]
    mid_ref[...] = mid
    unit, unused = norm_parts(mid)
    mlp_in_ref[...] = (unit * vec_ref[6:7, :] + vec_ref[7:8, :]).astype(jnp.bfloat16)
    copies[1].wait()
    copies[2].wait()
    mlp_ref[...] = jnp.broadcast_to(vec_ref[8:9, :], mlp_ref.shape)

    def feed(j):
        cols = pl.ds(pl.multiple_of(j * D, TILE), D)
        pre = dot_nn(mlp_in_ref[...], up_buf[:, cols]) + fc_ref[:, cols]
        pre_ref[:, cols] = pre
        act = (0.5 * pre * (1.0 + lax.erf(pre * (0.5**0.5)))).astype(jnp.bfloat16)
        act_ref[:, cols] = act
        mlp_ref[...] += dot_nt(act, down_buf[:, cols])

    loop(FF // D, feed)
    next_ref[...] = mid_ref[...] + vec_ref[9:10, :] * mlp_ref[...]


def head_kernel(
    images, slots, x_ref, special_ref, spots_ref, targets_ref, weight_ref, valid_ref, table_hbm,
    loss_ref, up_ref, gain_ref, shift_ref, picked_ref, picked_t_ref, d_logits_ref,
    table_buf, logits_ref, dpick_ref, sems,
):
    chunk = 1024
    number = table_hbm.shape[1] // chunk
    per = slots // images
    copies = [
        load(
            table_hbm.at[:, pl.ds(j * chunk, chunk)],
            table_buf.at[:, pl.ds(j * chunk, chunk)],
            sems.at[j],
        )
        for j in range(number)
    ]
    unit, unused = norm_parts(x_ref[...])
    normed = (unit * special_ref[2:3, :] + special_ref[3:4, :]).astype(jnp.bfloat16)
    hots = []
    for image in range(images):
        spots = spots_ref[pl.ds(image * per, per), :]
        hots.append((spots == iota((per, IMG), 1)).astype(jnp.bfloat16))
        picked_ref[pl.ds(image * per, per), :] = dot_nn(
            hots[image], normed[image * IMG : (image + 1) * IMG]
        ).astype(jnp.bfloat16)
    picked = picked_ref[...]
    high = jnp.full((slots, 1), -1e30, jnp.float32)
    for j in range(number):
        cols = pl.ds(j * chunk, chunk)
        copies[j].wait()
        part = dot_nn(picked, table_buf[:, cols])
        logits_ref[:, cols] = part
        high = jnp.maximum(high, jnp.max(part, 1, keepdims=True))
    total = jnp.zeros((slots, 1), jnp.float32)
    target = jnp.zeros((slots, 1), jnp.float32)
    for j in range(number):
        part = logits_ref[:, pl.ds(j * chunk, chunk)]
        total += jnp.sum(jnp.exp(part - high), 1, keepdims=True)
        hit = targets_ref[...] == iota((slots, chunk), 1) + j * chunk
        target += jnp.sum(jnp.where(hit, part, 0.0), 1, keepdims=True)
    log_total = high + jnp.log(total)
    loss_ref[...] = jnp.broadcast_to(
        col_sum((log_total - target) * valid_ref[...]), loss_ref.shape
    )
    dpick_ref[...] = jnp.zeros_like(dpick_ref)
    for j in range(number):
        cols = pl.ds(j * chunk, chunk)
        hit = targets_ref[...] == iota((slots, chunk), 1) + j * chunk
        d_part = (
            (jnp.exp(logits_ref[:, cols] - log_total) - jnp.where(hit, 1.0, 0.0)) * weight_ref[...]
        ).astype(jnp.bfloat16)
        d_logits_ref[:, cols] = d_part
        dpick_ref[...] += dot_nt(d_part, table_buf[:, cols])
    normed_grads = []
    for image in range(images):
        d_part = dpick_ref[pl.ds(image * per, per), :]
        normed_grads.append(sum(dot_tn(hots[image], part) for part in three_parts(d_part)))
    upstream, gain, shift = norm_backward(
        jnp.concatenate(normed_grads, 0), x_ref[...], special_ref[2:3, :]
    )
    up_ref[...] = upstream
    gain_ref[...] = gain
    shift_ref[...] = shift
    picked_t_ref[...] = picked.T


def backward_kernel(
    members, images, up_ref, x_ref, vec_ref, rel_ref, proj_ref, mixed_ref, attn_out_ref, mid_ref,
    mlp_in_ref, mlp_ref, pre_hbm, attn_hbm, up_hbm, down_hbm,
    next_ref, vec_grad_ref, fc_grad_ref, proj_grad_ref, sums_ref, d_pre_ref, d_cat_ref,
    attn_in_t_ref, g_attn_t_ref, mlp_in_t_ref, g_mlp_t_ref,
    attn_buf, up_buf, down_buf, pre_buf, acc_ref, mid_grad_ref, sems,
):
    copies = [
        load(src, dst, sems.at[i])
        for i, (src, dst) in enumerate(
            ((down_hbm, down_buf), (pre_hbm, pre_buf), (up_hbm, up_buf), (attn_hbm, attn_buf))
        )
    ]
    bf = jnp.bfloat16
    upstream = up_ref[...]
    g_mlp = (vec_ref[9:10, :] * upstream).astype(bf)
    g_mlp_t_ref[...] = g_mlp.T
    vec_grad_ref[9:10, :] = col_sum(upstream * mlp_ref[...])
    vec_grad_ref[8:9, :] = col_sum(g_mlp.astype(jnp.float32))
    mlp_in_t_ref[...] = mlp_in_ref[...].T
    acc_ref[...] = jnp.zeros_like(acc_ref)
    for copy in copies[:3]:
        copy.wait()

    def feed(j):
        cols = pl.ds(pl.multiple_of(j * D, TILE), D)
        pre = pre_buf[:, cols]
        slope = 0.5 * (1.0 + lax.erf(pre * (0.5**0.5))) + pre * jnp.exp(-0.5 * pre * pre) * (
            (2.0 * jnp.pi) ** (-0.5)
        )
        d_pre = (dot_nn(g_mlp, down_buf[:, cols]) * slope).astype(bf)
        d_pre_ref[:, cols] = d_pre
        fc_grad_ref[:, cols] = col_sum(d_pre.astype(jnp.float32))
        acc_ref[...] += dot_nt(d_pre, up_buf[:, cols])

    loop(FF // D, feed)
    d_mid, gain, shift = norm_backward(acc_ref[...], mid_ref[...], vec_ref[6:7, :])
    vec_grad_ref[6:7, :] = gain
    vec_grad_ref[7:8, :] = shift
    d_mid = d_mid + up_ref[...]
    mid_grad_ref[...] = d_mid
    g_attn = (vec_ref[5:6, :] * d_mid).astype(bf)
    g_attn_t_ref[...] = g_attn.T
    vec_grad_ref[5:6, :] = col_sum(d_mid * attn_out_ref[...])
    vec_grad_ref[4:5, :] = col_sum(g_attn.astype(jnp.float32))
    acc_ref[...] = jnp.zeros_like(acc_ref)
    copies[3].wait()

    def body(m):
        d_mixed = dot_nn(g_attn, attn_buf[:, member_cols(m, 4, 2)]).astype(bf)
        for image in range(images):
            rows = pl.ds(image * IMG, IMG)
            d_value, d_query, d_key = [], [], []
            for k in range(3):
                qt, kt, vt, ot, qk_half, vo_half = head_views(k)
                probs, query, key = head_probs(proj_ref, rel_ref, m, image, k)
                value = tile_of(proj_ref, m, image, vt)
                d_out = keep_half(
                    d_mixed[image * IMG : (image + 1) * IMG, ot * TILE : (ot + 1) * TILE], vo_half
                )
                d_value.append(dot_tn(probs.astype(bf), d_out))
                d_probs = dot_nt(d_out, value)
                d_scores = (
                    probs * (d_probs - jnp.sum(probs * d_probs, -1, keepdims=True))
                ).astype(bf)
                if image:
                    sums_ref[3 * m + k] += d_scores.astype(jnp.float32)
                else:
                    sums_ref[3 * m + k] = d_scores.astype(jnp.float32)
                d_query.append(dot_nn(d_scores, keep_half(key, qk_half)) * (DH ** (-0.5)))
                d_key.append(dot_tn(d_scores, query) * (DH ** (-0.5)))
            tiles = (
                d_query[0] + d_query[1],
                d_key[0] + d_key[1],
                d_value[0] + d_value[1],
                d_query[2] + d_value[2],
                d_key[2],
                jnp.zeros((IMG, TILE), jnp.float32),
            )
            for t, tile in enumerate(tiles):
                d_cat_ref[m, rows, pl.ds(t * TILE, TILE)] = tile.astype(bf)
        d_cat = d_cat_ref[m]
        proj_grad_ref[:, member_cols(m, 0, 6)] = col_sum(d_cat.astype(jnp.float32))
        acc_ref[...] += dot_nt(d_cat[:, : 5 * TILE], attn_buf[:, member_cols(m, 0, 5)])

    loop(members, body)
    d_input, gain, shift = norm_backward(acc_ref[...], x_ref[...], vec_ref[0:1, :])
    vec_grad_ref[0:1, :] = gain
    vec_grad_ref[1:2, :] = shift
    vec_grad_ref[2:4, :] = jnp.zeros((2, D), jnp.float32)
    next_ref[...] = d_input + mid_grad_ref[...]
    unit, unused = norm_parts(x_ref[...])
    attn_in = (unit * vec_ref[0:1, :] + vec_ref[1:2, :]).astype(bf)
    attn_in_t_ref[...] = attn_in.T


VMEM_SPEC = pl.BlockSpec(memory_space=pltpu.VMEM)
ANY_SPEC = pl.BlockSpec(memory_space=pl.ANY)
COMPUTE_PARAMS = pltpu.CompilerParams(vmem_limit_bytes=60 * 2**20)


def shaped(shape, kind=jnp.float32):
    return jax.ShapeDtypeStruct(shape, kind)


def embed(codes, kind, special, table, members, images):
    rows = images * IMG
    chunk = 1024
    return pl.pallas_call(
        functools.partial(embed_kernel, members, images),
        out_shape=shaped((rows, D)),
        in_specs=[VMEM_SPEC] * 3 + [ANY_SPEC],
        out_specs=VMEM_SPEC,
        scratch_shapes=[pltpu.VMEM((2, D, chunk), jnp.bfloat16), pltpu.SemaphoreType.DMA((2,))],
        compiler_params=COMPUTE_PARAMS,
        name="embed",
    )(codes, kind, special, table)


def forward_layer(x, vec, fc, proj_bias, rel, mats, members, images):
    rows = images * IMG
    bf = jnp.bfloat16
    return pl.pallas_call(
        functools.partial(forward_kernel, members, images),
        out_shape=[
            shaped((rows, D)),
            shaped((members, rows, 5 * TILE), bf),
            shaped((members, rows, 2 * TILE), bf),
            shaped((rows, D)),
            shaped((rows, D)),
            shaped((rows, D), bf),
            shaped((rows, FF)),
            shaped((rows, FF), bf),
            shaped((rows, D)),
        ],
        in_specs=[VMEM_SPEC] * 5 + [ANY_SPEC] * 3,
        out_specs=[VMEM_SPEC] * 9,
        scratch_shapes=[pltpu.VMEM((D, 4 * D), bf)] * 3 + [pltpu.SemaphoreType.DMA((3,))],
        compiler_params=COMPUTE_PARAMS,
        name="forward_layer",
    )(x, vec, fc, proj_bias, rel, *mats)


def head_and_loss(x, special, spots, targets, weight, valid, table, images):
    rows = images * IMG
    slots = spots.shape[0]
    bf = jnp.bfloat16
    return pl.pallas_call(
        functools.partial(head_kernel, images, slots),
        out_shape=[
            shaped((8, TILE)),
            shaped((rows, D)),
            shaped((1, D)),
            shaped((1, D)),
            shaped((slots, D), bf),
            shaped((D, slots), bf),
            shaped((slots, V), bf),
        ],
        in_specs=[VMEM_SPEC] * 6 + [ANY_SPEC],
        out_specs=[VMEM_SPEC] * 7,
        scratch_shapes=[
            pltpu.VMEM((D, V), bf),
            pltpu.VMEM((slots, V), jnp.float32),
            pltpu.VMEM((slots, D), jnp.float32),
            pltpu.SemaphoreType.DMA((V // 1024,)),
        ],
        compiler_params=COMPUTE_PARAMS,
        name="head_and_loss",
    )(x, special, spots, targets, weight, valid, table)


def backward_layer(upstream, x, vec, rel, kept, mats, members, images):
    rows = images * IMG
    bf = jnp.bfloat16
    proj, mixed, attn_out, mid, mlp_in, pre, mlp = kept
    attn_mat, up_mat, down_mat = mats
    return pl.pallas_call(
        functools.partial(backward_kernel, members, images),
        out_shape=[
            shaped((rows, D)),
            shaped((10, D)),
            shaped((1, FF)),
            shaped((1, 4 * D)),
            shaped((H, IMG, IMG)),
            shaped((rows, FF), bf),
            shaped((members, rows, 6 * TILE), bf),
            shaped((D, rows), bf),
            shaped((D, rows), bf),
            shaped((D, rows), bf),
            shaped((D, rows), bf),
        ],
        in_specs=[VMEM_SPEC] * 10 + [ANY_SPEC] * 4,
        out_specs=[VMEM_SPEC] * 11,
        scratch_shapes=[pltpu.VMEM((D, 4 * D), bf)] * 3
        + [
            pltpu.VMEM((rows, FF), jnp.float32),
            pltpu.VMEM((rows, D), jnp.float32),
            pltpu.VMEM((rows, D), jnp.float32),
            pltpu.SemaphoreType.DMA((4,)),
        ],
        compiler_params=COMPUTE_PARAMS,
        name="backward_layer",
    )(upstream, x, vec, rel, proj, mixed, attn_out, mid, mlp_in, mlp, pre, attn_mat, up_mat, down_mat)


def factor(ndp):
    half = ndp // 2
    inner = 1
    while inner * inner < half:
        inner *= 2
    return half // inner, inner


class Place:
    def __init__(self, outer, inner, members):
        index = lax.axis_index("dp")
        self.sizes = {"a": outer, "b": inner, "c": 2, "m": members}
        self.at = {
            "a": lax.div(index, 2 * inner),
            "b": lax.rem(lax.div(index, 2), inner),
            "c": lax.rem(index, 2),
            "m": lax.axis_index("mp"),
        }

    def shifted(self, axis, step):
        size = self.sizes[axis]
        return lax.rem(self.at[axis] + (step + size) % size, size)

    def device(self, axis, step):
        spot = dict(self.at)
        spot[axis] = self.shifted(axis, step)
        return ((spot["a"] * self.sizes["b"] + spot["b"]) * 2 + spot["c"], spot["m"])

    def enter(self):
        barrier = pltpu.get_barrier_semaphore()
        total = 0
        for axis, size in self.sizes.items():
            for step in range(1, size):
                pl.semaphore_signal(
                    barrier, inc=1, device_id=self.device(axis, step), device_id_type=MESH
                )
                total += 1
        pl.semaphore_wait(barrier, total)


def gather_kernel(outer, inner, members, groups, count, look, *refs):
    ins = refs[:count]
    outs = refs[count : 2 * count]
    send, recv, own = refs[2 * count :]
    place = Place(outer, inner, members)
    a, b, c, m = (place.at[axis] for axis in "abcm")
    place.enter()
    used = [0]

    def copies(piece, stage):
        i, first_row, rows, order = piece
        out = outs[i]
        width = ins[i].shape[1]
        span = pl.ds(first_row, rows)
        if stage == 0:
            axis, src = "m", ins[i].at[span]
            dst = out.at[a, b, c, span, pl.ds(pl.multiple_of(m * width, 128), width)]
        elif stage == 3:
            axis, src = "c", out.at[:, :, c, span]
            dst = src
        else:
            axis = order[stage - 1]
            if stage == 1:
                src = out.at[a, b, c, span]
            elif axis == "a":
                src = out.at[a, :, c, span]
            else:
                src = out.at[:, b, c, span]
            dst = src
        made = []
        for step in range(1, place.sizes[axis]):
            k = used[0]
            used[0] += 1
            made.append(
                pltpu.make_async_remote_copy(
                    src_ref=src,
                    dst_ref=dst,
                    send_sem=send.at[k],
                    recv_sem=recv.at[k],
                    device_id=place.device(axis, step),
                    device_id_type=MESH,
                )
            )
        return made

    flying = {}

    def start(group, stage):
        made = [copy for piece in groups[group] for copy in copies(piece, stage)]
        for copy in made:
            copy.start()
        flying[group, stage] = made

    total = len(groups)
    for group in range(min(look, total)):
        start(group, 0)
    local = []
    for i in range(count):
        width = ins[i].shape[1]
        mine = pl.ds(pl.multiple_of(m * width, 128), width)
        local.append(pltpu.make_async_copy(ins[i], outs[i].at[a, b, c, :, mine], own.at[i]))
    for copy in local:
        copy.start()
    for copy in local:
        copy.wait()
    for tick in range(total + 3):
        if tick + look < total:
            start(tick + look, 0)
        for stage in (2, 1, 0, 3):
            group = tick - stage
            if 0 <= group < total:
                for copy in flying[group, stage]:
                    copy.wait_recv()
                if stage < 3:
                    start(group, stage + 1)
    for made in flying.values():
        for copy in made:
            copy.wait_send()


def gather_blocks(blocks, ndp, members):
    outer, inner = factor(ndp)
    groups = []
    for i, block in enumerate(blocks):
        rows = block.shape[0]
        if rows % 32:
            groups.append([(i, 0, rows, "ab")])
        else:
            groups.append([(i, 0, rows // 2, "ab"), (i, rows // 2, rows // 2, "ba")])
    count = len(blocks)
    peers = (outer - 1) + (inner - 1) + 1 + (members - 1)
    sems = sum(len(group) for group in groups) * peers
    return pl.pallas_call(
        functools.partial(gather_kernel, outer, inner, members, groups, count, 2),
        out_shape=[
            jax.ShapeDtypeStruct((outer, inner, 2, x.shape[0], members * x.shape[1]), x.dtype)
            for x in blocks
        ],
        in_specs=[pl.BlockSpec(memory_space=pl.ANY)] * count,
        out_specs=[pl.BlockSpec(memory_space=pl.ANY)] * count,
        scratch_shapes=[
            pltpu.SemaphoreType.DMA((sems,)),
            pltpu.SemaphoreType.DMA((sems,)),
            pltpu.SemaphoreType.DMA((count,)),
        ],
        compiler_params=pltpu.CompilerParams(collective_id=0, has_side_effects=True),
        name="gather_blocks",
    )(*blocks)


class Channel:
    def __init__(self, place, axis, slots, total, send, recv, free):
        self.place, self.axis, self.slots, self.total = place, axis, slots, total
        self.send_sem, self.recv_sem, self.free = send, recv, free
        self.steps = range(1, place.sizes[axis])
        self.made = {}

    def before_fill(self, turn):
        if turn >= self.slots:
            for copy in self.made[turn - self.slots]:
                copy.wait_send()

    def send(self, turn, pairs):
        slot = turn % self.slots
        self.made[turn] = []
        for step, (src, dst) in zip(self.steps, pairs):
            if turn >= self.slots:
                pl.semaphore_wait(self.free.at[step - 1], 1)
            copy = pltpu.make_async_remote_copy(
                src_ref=src,
                dst_ref=dst,
                send_sem=self.send_sem.at[slot, step - 1],
                recv_sem=self.recv_sem.at[slot, step - 1],
                device_id=self.place.device(self.axis, step),
                device_id_type=MESH,
            )
            copy.start()
            self.made[turn].append(copy)

    def receive(self, turn):
        for copy in self.made[turn]:
            copy.wait_recv()

    def consumed(self, turn):
        if turn + self.slots < self.total:
            for step in self.steps:
                pl.semaphore_signal(
                    self.free.at[step - 1],
                    inc=1,
                    device_id=self.place.device(self.axis, -step),
                    device_id_type=MESH,
                )

    def drain(self):
        for turn in range(max(0, self.total - self.slots), self.total):
            for copy in self.made[turn]:
                copy.wait_send()


def reduce_kernel(outer, inner, members, rows, halves, groups, counts, lags, *refs):
    left_count, right_count, arrays = counts
    refs = list(refs)

    def take(number):
        taken = refs[:number]
        del refs[:number]
        return taken

    small_in, codes = take(2)
    lefts = take(left_count)
    rights = take(right_count)
    outs = take(arrays)
    small_out, square_out = take(2)
    right_bufs = take(2)
    (right_sem,) = take(1)
    sent0, got0, own0 = take(3)
    sent1a, got1a, keep1a, sent1b, got1b, keep1b = take(6)
    sent2a, got2a, sent2b, got2b, keep2 = take(5)
    sent3, got3 = take(2)
    sems = [take(3) for _ in range(6)]
    small_bufs = take(4)
    square_bufs = take(4)
    tiny_send, tiny_recv = take(2)

    place = Place(outer, inner, members)
    a, b, c, m = (place.at[axis] for axis in "abcm")
    total = len(groups)
    top, low_rows = halves
    lag1, lag2, lag3, lag4 = lags
    slots = (2, lag2 - lag1, lag3 - lag2, lag4 - lag3)
    chan0 = Channel(place, "c", slots[0], total, *sems[0])
    chan1a = Channel(place, "a", slots[1], total, *sems[1])
    chan1b = Channel(place, "b", slots[1], total, *sems[2])
    chan2a = Channel(place, "b", slots[2], total, *sems[3])
    chan2b = Channel(place, "a", slots[2], total, *sems[4])
    chan3 = Channel(place, "m", slots[3], total, *sems[5])
    channels = [chan0, chan1a, chan2a, chan3]
    if low_rows:
        channels += [chan1b, chan2b]

    def each_member(body):
        def step(i, unused):
            body(i)
            return 0

        lax.fori_loop(0, members, step, 0)

    def fetch(turn):
        width = groups[turn][2]
        copies = []
        for j, (left, right, first, block) in enumerate(groups[turn][3]):
            if right is None:
                continue
            ref = rights[right]
            depth = ref.shape[-2]
            for k in range(members):
                if len(ref.shape) == 3:
                    src = ref.at[k, :, pl.ds(first, width)]
                else:
                    src = ref.at[:, pl.ds(k * block + first, width)]
                copies.append(
                    pltpu.make_async_copy(
                        src,
                        right_bufs[j].at[turn % 2, k, pl.ds(0, depth), pl.ds(0, width)],
                        right_sem.at[turn % 2, j, k],
                    )
                )
        return copies

    def product(turn, half, k):
        width = groups[turn][2]
        total = None
        for j, (left, right, first, block) in enumerate(groups[turn][3]):
            ref = lefts[left]
            x = ref[:, half].reshape(outer * inner * rows, ref.shape[-1])
            if right is None:
                spot = lax.broadcasted_iota(jnp.int32, (codes.shape[0], width), 1) + (
                    k * block + first
                )
                y = (codes[...] == spot).astype(jnp.bfloat16)
            else:
                y = right_bufs[j][turn % 2, k, pl.ds(0, rights[right].shape[-2]), pl.ds(0, width)]
            part = jnp.dot(x, y, preferred_element_type=jnp.float32)
            total = part if total is None else total + part
        return total.reshape(outer, inner, rows, width)

    def make(turn):
        i, first, width = groups[turn][:3]
        cols = pl.ds(0, width)
        slot = turn % 2
        for copy in fetch(turn):
            copy.wait()
        if turn + 1 < total:
            for copy in fetch(turn + 1):
                copy.start()
        chan0.before_fill(turn)

        def fill(k):
            sent0[slot, k, :, :, :, cols] = product(turn, 1 - c, k).astype(jnp.bfloat16)

        each_member(fill)
        chan0.send(
            turn, [(sent0.at[slot, :, :, :, :, cols], got0.at[slot, :, :, :, :, cols])]
        )

        def fill_own(k):
            own0[slot, k, :, :, :, cols] = product(turn, c, k)

        each_member(fill_own)

    def stage_one(turn):
        i, first, width = groups[turn][:3]
        cols = pl.ds(0, width)
        old, new = turn % 2, turn % slots[1]
        upper, lower = pl.ds(0, top), pl.ds(top, low_rows)
        chan1a.before_fill(turn)
        if low_rows:
            chan1b.before_fill(turn)
        chan0.receive(turn)

        def body(k):
            for step in range(outer):
                part = place.shifted("a", step)
                summed = own0[old, k, part, :, upper, cols] + got0[
                    old, k, part, :, upper, cols
                ].astype(jnp.float32)
                if step:
                    sent1a[new, step - 1, k, :, :, cols] = summed.astype(jnp.bfloat16)
                else:
                    keep1a[new, k, :, :, cols] = summed
            if low_rows:
                for step in range(inner):
                    part = place.shifted("b", step)
                    summed = own0[old, k, :, part, lower, cols] + got0[
                        old, k, :, part, lower, cols
                    ].astype(jnp.float32)
                    if step:
                        sent1b[new, step - 1, k, :, :, cols] = summed.astype(jnp.bfloat16)
                    else:
                        keep1b[new, k, :, :, cols] = summed

        each_member(body)
        chan0.consumed(turn)
        chan1a.send(
            turn,
            [
                (sent1a.at[new, j, :, :, :, cols], got1a.at[new, j, :, :, :, cols])
                for j in range(outer - 1)
            ],
        )
        if low_rows:
            chan1b.send(
                turn,
                [
                    (sent1b.at[new, j, :, :, :, cols], got1b.at[new, j, :, :, :, cols])
                    for j in range(inner - 1)
                ],
            )

    def stage_two(turn):
        i, first, width = groups[turn][:3]
        cols = pl.ds(0, width)
        old, new = turn % slots[1], turn % slots[2]
        chan2a.before_fill(turn)
        if low_rows:
            chan2b.before_fill(turn)
        chan1a.receive(turn)
        if low_rows:
            chan1b.receive(turn)

        def body(k):
            for step in range(inner):
                part = place.shifted("b", step)
                summed = keep1a[old, k, part, :, cols]
                for j in range(outer - 1):
                    summed += got1a[old, j, k, part, :, cols].astype(jnp.float32)
                if step:
                    sent2a[new, step - 1, k, :, cols] = summed.astype(jnp.bfloat16)
                else:
                    keep2[new, k, pl.ds(0, top), cols] = summed
            if low_rows:
                for step in range(outer):
                    part = place.shifted("a", step)
                    summed = keep1b[old, k, part, :, cols]
                    for j in range(inner - 1):
                        summed += got1b[old, j, k, part, :, cols].astype(jnp.float32)
                    if step:
                        sent2b[new, step - 1, k, :, cols] = summed.astype(jnp.bfloat16)
                    else:
                        keep2[new, k, pl.ds(top, low_rows), cols] = summed

        each_member(body)
        chan1a.consumed(turn)
        if low_rows:
            chan1b.consumed(turn)
        chan2a.send(
            turn,
            [
                (sent2a.at[new, j, :, :, cols], got2a.at[new, j, :, :, cols])
                for j in range(inner - 1)
            ],
        )
        if low_rows:
            chan2b.send(
                turn,
                [
                    (sent2b.at[new, j, :, :, cols], got2b.at[new, j, :, :, cols])
                    for j in range(outer - 1)
                ],
            )

    def stage_three(turn):
        i, first, width = groups[turn][:3]
        cols = pl.ds(0, width)
        old, new = turn % slots[2], turn % slots[3]
        chan3.before_fill(turn)
        chan2a.receive(turn)
        if low_rows:
            chan2b.receive(turn)

        def body(k):
            summed = keep2[old, k, pl.ds(0, top), cols]
            for j in range(inner - 1):
                summed += got2a[old, j, k, :, cols].astype(jnp.float32)
            sent3[new, k, pl.ds(0, top), cols] = summed
            if low_rows:
                summed = keep2[old, k, pl.ds(top, low_rows), cols]
                for j in range(outer - 1):
                    summed += got2b[old, j, k, :, cols].astype(jnp.float32)
                sent3[new, k, pl.ds(top, low_rows), cols] = summed

        each_member(body)
        chan2a.consumed(turn)
        if low_rows:
            chan2b.consumed(turn)
        chan3.send(
            turn,
            [
                (sent3.at[new, place.shifted("m", j + 1), :, cols], got3.at[new, j, :, cols])
                for j in range(members - 1)
            ],
        )

    def stage_four(turn):
        i, first, width = groups[turn][:3]
        cols = pl.ds(0, width)
        old = turn % slots[3]
        chan3.receive(turn)
        summed = sent3[old, m, :, cols]
        for j in range(members - 1):
            summed += got3[old, j, :, cols]
        outs[i][:, pl.ds(first, width)] = summed
        chan3.consumed(turn)

    tiny_used = [0]
    tiny_made = []

    def spread(buf, axis):
        made = []
        entry = buf.at[place.at[axis]]
        for step in range(1, place.sizes[axis]):
            k = tiny_used[0]
            tiny_used[0] += 1
            copy = pltpu.make_async_remote_copy(
                src_ref=entry,
                dst_ref=entry,
                send_sem=tiny_send.at[k],
                recv_sem=tiny_recv.at[k],
                device_id=place.device(axis, step),
                device_id_type=MESH,
            )
            copy.start()
            made.append(copy)
        tiny_made.extend(made)
        return made

    def sum_entries(buf, made):
        for copy in made:
            copy.wait_recv()
        summed = buf[0]
        for k in range(1, buf.shape[0]):
            summed += buf[k]
        return summed

    place.enter()
    for copy in fetch(0):
        copy.start()
    small_made = [None] * 4
    for tick in range(total + lag4):
        if lag4 <= tick:
            stage_four(tick - lag4)
        if 0 <= tick - lag3 < total:
            stage_three(tick - lag3)
        if 0 <= tick - lag2 < total:
            stage_two(tick - lag2)
        if 0 <= tick - lag1 < total:
            stage_one(tick - lag1)
        if tick < total:
            make(tick)
        if tick in (1, 3, 5, 7, 9):
            hop = (tick - 1) // 2
            value = small_in[...] if hop == 0 else sum_entries(small_bufs[hop - 1], small_made[hop - 1])
            if hop == 4:
                small_out[...] = value
            else:
                axis = "cabm"[hop]
                small_bufs[hop][place.at[axis]] = value
                small_made[hop] = spread(small_bufs[hop], axis)
    for channel in channels:
        channel.drain()
    value = jnp.zeros((8, 128), jnp.float32)
    for i in range(arrays):
        block = outs[i][...]
        value += jnp.sum((block * block).reshape(-1, 8, 128), 0) if block.shape[1] == 128 else sum_tiles(block)
    for hop, axis in enumerate("cabm"):
        square_bufs[hop][place.at[axis]] = value
        value = sum_entries(square_bufs[hop], spread(square_bufs[hop], axis))
    square_out[...] = value
    for copy in tiny_made:
        copy.wait_send()


def sum_tiles(block):
    squares = block * block
    folded = squares[:8]
    for first in range(8, block.shape[0], 8):
        folded += squares[first : first + 8]
    total = folded[:, :128]
    for first in range(128, block.shape[1], 128):
        total += folded[:, first : first + 128]
    return total


def reduce_products(lefts, rights, codes, arrays, small, ndp, members):
    outer, inner = factor(ndp)
    per_device = D // ndp
    rows = -(-per_device // 16) * 16
    halves = (rows // 2, rows // 2) if rows % 32 == 0 else (rows, 0)
    top, low_rows = halves
    low_shape = max(low_rows, 16)
    lags = (1, 3, 5, 7)
    slots = (2, 2, 2, 2)
    spread_lefts = []
    for x in lefts:
        x = x.reshape(outer * inner, 2, per_device, x.shape[1])
        spread_lefts.append(jnp.pad(x, ((0, 0), (0, 0), (0, rows - per_device), (0, 0))))
    groups, outs = [], []
    for i, (block, cuts) in enumerate(arrays):
        outs.append(jax.ShapeDtypeStruct((rows, block), jnp.float32))
        groups += [(i,) + cut for cut in cuts]
    most = max(group[2] for group in groups)
    deepest, seconds = 16, (16, TILE)
    for group in groups:
        for j, part in enumerate(group[3]):
            if part[1] is None:
                continue
            depth = rights[part[1]].shape[-2]
            if j:
                seconds = (max(seconds[0], depth), max(seconds[1], group[2]))
            else:
                deepest = max(deepest, depth)
    counts = (len(lefts), len(rights), len(arrays))
    small_shape = small.shape
    bf, f4 = jnp.bfloat16, jnp.float32
    mem = pltpu.VMEM
    scratch = [
        mem((2, members, deepest, most), bf),
        mem((2, members) + seconds, bf),
        pltpu.SemaphoreType.DMA((2, 2, members)),
        mem((slots[0], members, outer, inner, rows, most), bf),
        mem((slots[0], members, outer, inner, rows, most), bf),
        mem((2, members, outer, inner, rows, most), f4),
        mem((slots[1], outer - 1, members, inner, top, most), bf),
        mem((slots[1], outer - 1, members, inner, top, most), bf),
        mem((slots[1], members, inner, top, most), f4),
        mem((slots[1], inner - 1, members, outer, low_shape, most), bf),
        mem((slots[1], inner - 1, members, outer, low_shape, most), bf),
        mem((slots[1], members, outer, low_shape, most), f4),
        mem((slots[2], inner - 1, members, top, most), bf),
        mem((slots[2], inner - 1, members, top, most), bf),
        mem((slots[2], outer - 1, members, low_shape, most), bf),
        mem((slots[2], outer - 1, members, low_shape, most), bf),
        mem((slots[2], members, rows, most), f4),
        mem((slots[3], members, rows, most), f4),
        mem((slots[3], members - 1, rows, most), f4),
    ]
    for depth, size in zip((0, 1, 1, 2, 2, 3), (2, outer, inner, inner, outer, members)):
        scratch += [
            pltpu.SemaphoreType.DMA((slots[depth], size - 1)),
            pltpu.SemaphoreType.DMA((slots[depth], size - 1)),
            pltpu.SemaphoreType.REGULAR((size - 1,)),
        ]
    sizes = (2, outer, inner, members)
    scratch += [mem((size,) + small_shape, f4) for size in sizes]
    scratch += [mem((size, 8, 128), f4) for size in sizes]
    tiny = 2 * sum(size - 1 for size in sizes)
    scratch += [pltpu.SemaphoreType.DMA((tiny,)), pltpu.SemaphoreType.DMA((tiny,))]
    vmem = pl.BlockSpec(memory_space=pltpu.VMEM)
    results = pl.pallas_call(
        functools.partial(
            reduce_kernel, outer, inner, members, rows, halves, groups, counts, lags
        ),
        out_shape=outs
        + [jax.ShapeDtypeStruct(small_shape, f4), jax.ShapeDtypeStruct((8, 128), f4)],
        in_specs=[vmem] * (2 + counts[0]) + [pl.BlockSpec(memory_space=pl.ANY)] * counts[1],
        out_specs=[vmem] * (counts[2] + 2),
        scratch_shapes=scratch,
        compiler_params=pltpu.CompilerParams(
            collective_id=1, has_side_effects=True, vmem_limit_bytes=62 * 2**20
        ),
        name="reduce_products",
    )(small, codes, *spread_lefts, *rights)
    return [block[:per_device] for block in results[:-2]], results[-2], results[-1]


def local(members, ndp, *args):
    (
        qkv_weight, qkv_first, qkv_second,
        out_weight, out_first, out_second,
        up_weight, up_first, up_second,
        down_weight, down_first, down_second,
        code_table, table_first, table_second,
        small_params, small_first, small_second,
        patch_codes, masked_pos, masked_count,
    ) = args
    bf, f4 = jnp.bfloat16, jnp.float32
    member = lax.axis_index("mp")
    images = patch_codes.shape[0] // members
    width_part = D // members
    vectors, fc_bias, rel_tables, special = unpack_small(small_params)

    blocks = []
    count_here = jnp.full((8, 128), jnp.sum(masked_count).astype(f4))
    part = 2 * DH
    for l in range(LAYERS):
        wq, wk, wv, wo = qkv_weight[l, 0], qkv_weight[l, 1], qkv_weight[l, 2], out_weight[l].T
        blocks.append(
            jnp.concatenate(
                [wq[:, :part], wk[:, :part], wv[:, :part], wq[:, part:], wv[:, part:],
                 wk[:, part:], wo[:, part:], wo[:, :part]],
                1,
            ).astype(bf)
        )
        blocks.append(up_weight[l].astype(bf))
        blocks.append(down_weight[l].T.astype(bf))
    blocks = [blocks[0], code_table.T.astype(bf)] + blocks[1:] + [count_here]
    gathered = list(gather_blocks(blocks, ndp, members))
    counts_all = gathered.pop()
    mats = [g.reshape(D, g.shape[-1]) for g in gathered]
    table = mats.pop(1)
    layer_mats = [mats[3 * l : 3 * l + 3] for l in range(LAYERS)]
    count_total = jnp.sum(counts_all.reshape(ndp, 8, members * 128)[:, 0, 0])
    inverse_total = jnp.ones((), f4) / count_total

    def mine(values):
        return lax.dynamic_slice_in_dim(values, member * images, images, 0)

    image_codes = mine(patch_codes)
    masked_spots = mine(masked_pos)
    counts = mine(masked_count)
    valid_slots = jnp.arange(MAXM)[None, :] < counts[:, None]
    hidden_patch = jnp.any(
        (masked_spots[:, :, None] == jnp.arange(PATCH)[None, None, :]) & valid_slots[:, :, None], 1
    )
    token = jnp.arange(IMG)[None, :]

    def by_token(values, fill):
        return jnp.pad(values, ((0, 0), (1, IMG - SEQ)), constant_values=fill)

    masked_rows = by_token(hidden_patch, False)
    seen_rows = by_token(jnp.logical_not(hidden_patch), False)
    kind = jnp.where(seen_rows, 0, jnp.where(token == 0, 1, 2)).astype(jnp.int32).reshape(-1, 1)
    codes = jnp.where(seen_rows, by_token(image_codes, -1), -1).reshape(-1, 1)
    slot_pad = ((0, 0), (0, -MAXM % 16))
    targets = jnp.sum(
        jnp.where(
            masked_spots[:, :, None] == jnp.arange(PATCH)[None, None, :], image_codes[:, None, :], 0
        ),
        2,
    )
    targets = jnp.pad(targets, slot_pad, constant_values=-1).reshape(-1, 1)
    spots = jnp.pad(masked_spots + 1, slot_pad, constant_values=-1).reshape(-1, 1)
    valid_float = jnp.pad(valid_slots.astype(f4), slot_pad).reshape(-1, 1)
    row_weight = valid_float * inverse_total

    biases = rel_biases(rel_tables).reshape(LAYERS, H, IMG, IMG)
    x = embed(codes, kind, special, table, members, images)
    kept = []
    for l in range(LAYERS):
        vec = vectors[l]
        bias_q = vec[2].reshape(members, width_part)
        bias_v = vec[3].reshape(members, width_part)
        zeros = jnp.zeros((members, part), f4)
        proj_bias = jnp.concatenate(
            [bias_q[:, :part], zeros, bias_v[:, :part], bias_q[:, part:], bias_v[:, part:], zeros, zeros],
            1,
        ).reshape(1, 4 * D)
        following, proj, mixed, attn_out, mid, mlp_in, pre, act, mlp = forward_layer(
            x, vec, fc_bias[l][None], proj_bias, biases[l], layer_mats[l], members, images
        )
        kept.append((x, mixed, act, (proj, mixed, attn_out, mid, mlp_in, pre, mlp)))
        x = following
    loss_tile, upstream, d_gain, d_shift, picked, picked_t, d_logits = head_and_loss(
        x, special, spots, targets, row_weight, valid_float, table, images
    )
    loss_part = loss_tile[0, 0]
    lefts, rights, arrays = [], [], []
    vec_grads, fc_grads, sums = [None] * LAYERS, [None] * LAYERS, [None] * LAYERS

    def cuts_of(width, size, parts):
        return [
            (first, size, tuple((left, right, first, width) for left, right in parts))
            for first in range(0, width, size)
        ]

    for l in reversed(range(LAYERS)):
        x_in, mixed, act, rest = kept[l]
        (upstream, vec_grad, fc_grad, proj_grad, sums[l], d_pre, d_cat,
         attn_in_t, g_attn_t, mlp_in_t, g_mlp_t) = backward_layer(
            upstream, x_in, vectors[l], biases[l], rest, layer_mats[l], members, images
        )
        proj_grad = proj_grad.reshape(members, 6 * TILE)
        d_bias_q = jnp.concatenate([proj_grad[:, :part], proj_grad[:, 3 * part : 3 * part + DH]], 1)
        d_bias_v = jnp.concatenate(
            [proj_grad[:, 2 * part : 3 * part], proj_grad[:, 3 * part + DH : 4 * part]], 1
        )
        vec_grads[l] = jnp.concatenate(
            [vec_grad[:2], d_bias_q.reshape(1, D), d_bias_v.reshape(1, D), vec_grad[4:]], 0
        )
        fc_grads[l] = fc_grad[0]
        i, j = len(lefts), len(rights)
        lefts += [attn_in_t, g_attn_t, mlp_in_t, g_mlp_t]
        rights += [d_cat, mixed, d_pre, act]
        arrays += [
            (D, [(0, 512, ((i, j, 0, D),)), (512, 256, ((i, j, 512, D), (i + 1, j + 1, 0, 256)))]),
            (D, cuts_of(D, 384, ((i + 2, j + 2),))),
            (D, cuts_of(D, 384, ((i + 3, j + 3),))),
        ]
    cls_rows = jnp.broadcast_to(token == 0, (images, IMG)).reshape(-1, 1)
    d_cls = jnp.sum(jnp.where(cls_rows, upstream, 0.0), 0)
    d_mask = jnp.sum(jnp.where(masked_rows.reshape(-1, 1), upstream, 0.0), 0)
    seen_grad = jnp.where(seen_rows.reshape(-1, 1), upstream, 0.0).astype(bf)
    i = len(lefts)
    lefts += [picked_t, seen_grad.T]
    arrays.append((V // members, cuts_of(V // members, 512, ((i, len(rights)), (i + 1, None)))))
    rights.append(d_logits)
    small_grad = pack_small(
        jnp.stack(vec_grads), jnp.stack(fc_grads),
        rel_grads(jnp.concatenate(sums, 0)),
        jnp.stack([d_cls, d_mask, d_gain[0], d_shift[0]]),
    )
    small_size = small_grad.shape[0]
    packed = jnp.concatenate([small_grad, loss_part[None]])
    packed = jnp.pad(packed, (0, -packed.shape[0] % 1024)).reshape(-1, 128)

    grads, small_sum, squares = reduce_products(lefts, rights, codes, arrays, packed, ndp, members)
    grad_table = grads[-1].T
    by_layer = [grads[3 * (LAYERS - 1 - l) :][:3] for l in range(LAYERS)]

    def joined(g, first, second):
        return jnp.concatenate([g[:, first : first + part], g[:, second : second + DH]], 1)

    grad_qkv = jnp.stack(
        [
            jnp.stack(
                [
                    joined(g[0], 0, 3 * part),
                    joined(g[0], part, 4 * part),
                    joined(g[0], 2 * part, 3 * part + DH),
                ]
            )
            for g in by_layer
        ]
    )
    grad_out = jnp.stack([joined(g[0], 5 * part, 4 * part + DH).T for g in by_layer])
    grad_up = jnp.stack([g[1] for g in by_layer])
    grad_down = jnp.stack([g[2].T for g in by_layer])
    small_sum = small_sum.reshape(-1)
    grad_small = small_sum[:small_size]
    loss_total = small_sum[small_size]
    grad_norm = jnp.sqrt(jnp.sum(squares) + jnp.sum(grad_small * grad_small))
    factor_clip = jnp.minimum(1.0, CLIP_NORM / (grad_norm + 1e-06))
    results = ()
    for weight, one, two, grad, decay in (
        (qkv_weight, qkv_first, qkv_second, grad_qkv, WEIGHT_DECAY),
        (out_weight, out_first, out_second, grad_out, WEIGHT_DECAY),
        (up_weight, up_first, up_second, grad_up, WEIGHT_DECAY),
        (down_weight, down_first, down_second, grad_down, WEIGHT_DECAY),
        (code_table, table_first, table_second, grad_table, WEIGHT_DECAY),
        (small_params, small_first, small_second, grad_small, 0.0),
    ):
        results += adam_update(weight, one, two, grad, factor_clip, decay)
    return results + (loss_total, count_total, grad_norm)


def solution(mesh):
    in_specs = (
        P(None, None, "dp", "mp"),
        P(None, None, "dp", "mp"),
        P(None, None, "dp", "mp"),
        P(None, "mp", "dp"),
        P(None, "mp", "dp"),
        P(None, "mp", "dp"),
        P(None, "dp", "mp"),
        P(None, "dp", "mp"),
        P(None, "dp", "mp"),
        P(None, "mp", "dp"),
        P(None, "mp", "dp"),
        P(None, "mp", "dp"),
        P("mp", "dp"),
        P("mp", "dp"),
        P("mp", "dp"),
        P(),
        P(),
        P(),
        P("dp", None),
        P("dp", None),
        P("dp"),
    )
    out_specs = (
        P(None, None, "dp", "mp"),
        P(None, None, "dp", "mp"),
        P(None, None, "dp", "mp"),
        P(None, "mp", "dp"),
        P(None, "mp", "dp"),
        P(None, "mp", "dp"),
        P(None, "dp", "mp"),
        P(None, "dp", "mp"),
        P(None, "dp", "mp"),
        P(None, "mp", "dp"),
        P(None, "mp", "dp"),
        P(None, "mp", "dp"),
        P("mp", "dp"),
        P("mp", "dp"),
        P("mp", "dp"),
        P(),
        P(),
        P(),
        P(),
        P(),
        P(),
    )
    body = functools.partial(local, mesh.shape["mp"], mesh.shape["dp"])
    return jax.shard_map(body, mesh=mesh, in_specs=in_specs, out_specs=out_specs, check_vma=False)
```
